512 devices in a mesh: rep: 32 (over x, y_hi, core), fsdp: 16 (over y_lo, z).
Axes of the slice: x: 4, y: 8 (y_hi: 4, y_lo: 2; y = y_hi * 2 + y_lo), z: 8, core: 2. Of those that a mesh axis runs over, the one named last changes fastest.
Arguments:
- tokens: bfloat16 [32, 2048, 8192], P('rep', 'fsdp'), may hold values from -6 to 6
- norm_gain: float32 [8192], replicated, may hold values from 0.25 to 3
- weights: bfloat16 [32, 8192, 512], P('rep', 'fsdp'), may hold values from -0.0625 to 0.0625
- first_moment: bfloat16 [32, 8192, 512], P('rep', 'fsdp'), may hold values from -0.0078125 to 0.0078125
- second_moment: bfloat16 [32, 8192, 512], P('rep', 'fsdp'), may hold values from 9.9651515e-08 to 9.983778e-07
- upstream: bfloat16 [32, 2048, 512], P('rep', 'fsdp'), may hold values from -6 to 6
- global_params: float32 [4, 16, 512, 128], P(None, 'fsdp', 'rep'), may hold values from -0.0625 to 0.0625
- outer_momentum: float32 [4, 16, 512, 128], P(None, 'fsdp', 'rep'), may hold values from -0.078125 to 0.078125
- fragment: int32 [1], replicated, may hold values from 0 to 3
Outputs:
- new_weights: bfloat16 [32, 8192, 512], P('rep', 'fsdp')
- values: bfloat16 [32, 2048, 512], P('rep', 'fsdp')
- new_global: float32 [4, 16, 512, 128], P(None, 'fsdp', 'rep')
- new_momentum: float32 [4, 16, 512, 128], P(None, 'fsdp', 'rep')
The draws below stay inside these ranges and needn't reach their ends.
All inputs are finite; a program needn't handle non-finite values.
Results may differ from the reference program's by a relative error of at most 0.0049.
Values may be sent and summed in bfloat16 or wider, within the bound.
A program may use at most 64 MiB of HBM per device.

```python
import math
import jax
import jax.numpy as jnp
from jax import lax

D = 8192
HEAD = 128
KVW = 512
FRAGS = 4
REPLICAS = 32
SEQ = 2048
N_REP = 32
N_FSDP = 16


def draw_norm_gain(key, part):
    key = jax.random.fold_in(key, 11)
    place = jnp.arange(D).astype(jnp.float32) / (D - 1)
    base = 0.5 * (1.0 + 2.0 * place)
    rough = jax.random.uniform(key, (D,), jnp.float32, 0.7, 1.4)
    return (base * rough).astype(jnp.float32)


def levels(key, shape, cuts, smallest, largest):
    def one(dim, blocks):
        draws = jax.random.uniform(jax.random.fold_in(jax.random.fold_in(key, 6), dim), (blocks,), jnp.float32, smallest / len(cuts), largest / len(cuts))
        return jnp.repeat(jnp.exp(draws), shape[dim] // blocks).reshape((-1,) + (1,) * (len(shape) - dim - 1))

    level = one(*cuts[0])
    for cut in cuts[1:]:
        level = level * one(*cut)
    return level


def bell_draw(own_key, extent, deviation, most, cuts=(), dtype=jnp.bfloat16):
    loudness = levels(own_key, extent, cuts, -0.22, 0.18) if cuts else 1.0
    drawn = jax.random.normal(own_key, extent, jnp.float32) * deviation * loudness
    return jnp.minimum(jnp.maximum(drawn, -most), most).astype(dtype)


def setup_inputs(seed: int = 0) -> dict:
    arg_keys = jax.random.split(jax.random.key(seed), 10)
    return {
        "tokens": bell_draw(arg_keys[0], (REPLICAS, SEQ, D), 1.0, 6.0, ((0, 32), (1, 16))),
        "norm_gain": draw_norm_gain(jax.random.fold_in(arg_keys[9], 71), 0),
        "weights": bell_draw(arg_keys[2], (REPLICAS, D, KVW), D ** -0.5, 0.0625, ((0, 32), (1, 16))),
        "first_moment": bell_draw(arg_keys[3], (REPLICAS, D, KVW), 0.0005, 0.0078125, ((0, 32), (1, 16))),
        "second_moment": jnp.clip(jnp.exp(math.log(9.98377799987793e-07) - 2.3044525 * jax.random.uniform(arg_keys[4], (REPLICAS, D, KVW), jnp.float32) ** levels(arg_keys[4], (REPLICAS, D, KVW), ((0, 32), (1, 16)), -0.2, 0.2)), 9.96515154838562e-08, 9.98377799987793e-07).astype(jnp.bfloat16),
        "upstream": bell_draw(arg_keys[5], (REPLICAS, SEQ, KVW), 1.0, 6.0, ((0, 32), (1, 16))),
        "global_params": bell_draw(arg_keys[6], (FRAGS, N_FSDP, D // N_FSDP, HEAD), D ** -0.5, 0.0625, ((1, 16), (2, 32)), jnp.float32),
        "outer_momentum": bell_draw(arg_keys[7], (FRAGS, N_FSDP, D // N_FSDP, HEAD), 0.005, 0.078125, ((1, 16), (2, 32)), jnp.float32),
        "fragment": jax.random.randint(arg_keys[8], (1,), 0, FRAGS).astype(jnp.int32),
    }


clip_bound = 1.0
inner_rate = 0.02
decay_rate = 0.1
outer_rate = 0.7
outer_mom = 0.9
blend = 0.5

def one_replica(norm_gain, items):
    tokens, weights, first_moment, second_moment, upstream = items
    xf = tokens.astype(jnp.float32)
    scale = lax.rsqrt(lax.optimization_barrier(jnp.mean(xf * xf, axis=-1, keepdims=True)) + 1e-05)
    normed = (xf * scale * norm_gain).astype(jnp.bfloat16)
    values = jnp.dot(normed, weights, preferred_element_type=jnp.float32).astype(jnp.bfloat16)
    grad = jnp.dot(normed.T, upstream, preferred_element_type=jnp.float32)
    total = jnp.sum(grad * grad)
    factor = jnp.minimum(1.0, clip_bound / (jnp.sqrt(total) + 1e-06))
    clipped = factor * grad
    moment = 0.9 * first_moment.astype(jnp.float32) + 0.1 * clipped
    square = 0.95 * second_moment.astype(jnp.float32) + 0.05 * clipped * clipped
    wf = weights.astype(jnp.float32)
    inner = wf - inner_rate * (moment / (jnp.sqrt(square) + 1e-08) + decay_rate * wf)
    return (inner, values)

def reference(tokens, norm_gain, weights, first_moment, second_moment, upstream, global_params, outer_momentum, fragment):
    inner_all, values = lax.map(lambda items: one_replica(norm_gain, items), (tokens, weights, first_moment, second_moment, upstream))
    frag = fragment[0].astype(jnp.int32)
    start = (frag * HEAD).astype(jnp.int32)
    glob = global_params.reshape(FRAGS, D, HEAD)
    moms = outer_momentum.reshape(FRAGS, D, HEAD)
    g_frag = lax.dynamic_index_in_dim(glob, frag, 0, keepdims=False)
    u_frag = lax.dynamic_index_in_dim(moms, frag, 0, keepdims=False)
    old_cols = lax.dynamic_slice_in_dim(weights, start, HEAD, 2).astype(jnp.float32)
    summed = lax.optimization_barrier(jnp.sum(old_cols, axis=0))
    delta = g_frag - summed / N_REP
    u_new = outer_mom * u_frag + delta
    g_new = g_frag - outer_rate * (outer_mom * u_new + delta)
    merged = blend * lax.dynamic_slice_in_dim(inner_all, start, HEAD, 2) + (1.0 - blend) * g_new[None]
    new_weights = lax.dynamic_update_slice_in_dim(inner_all, merged, start, 2).astype(jnp.bfloat16)
    mask = (jnp.arange(FRAGS).astype(jnp.int32) == frag)[:, None, None]
    new_global = jnp.where(mask, g_new[None], glob).reshape(global_params.shape)
    new_momentum = jnp.where(mask, u_new[None], moms).reshape(outer_momentum.shape)
    return (new_weights, values, new_global, new_momentum)
```

```python
import functools

import jax
import jax.numpy as jnp
from jax import lax
from jax.experimental import pallas as pl
from jax.experimental.pallas import tpu as pltpu
from jax.sharding import PartitionSpec as P

MESH = pl.DeviceIdType.MESH

clip_bound = 1.0
inner_rate = 0.02
decay_rate = 0.1
outer_rate = 0.7
outer_mom = 0.9
blend = 0.5

ORDER = (1, 7, 2, 6, 3, 5, 4)


def kernel(
    n_rep,
    nz,
    tok_hbm,
    gain_ref,
    w_hbm,
    fm_hbm,
    sm_hbm,
    u_hbm,
    gp_ref,
    mom_ref,
    frag_ref,
    nw_hbm,
    val_hbm,
    ng_ref,
    nm_ref,
    x,
    tp,
    to,
    tg,
    wcat,
    ucat,
    fm,
    sm,
    nw,
    gown,
    gsend,
    grecv,
    vsend,
    vrecv,
    vown,
    vout,
    scale_ref,
    wsel,
    wrecv,
    gnew,
    grow,
    gfull,
    nsend,
    nrecv,
    loc,
    t_s,
    t_r,
    u_s,
    u_r,
    v_s,
    v_r,
    one_s,
    one_r,
):
    r = lax.axis_index("rep")
    f = lax.axis_index("fsdp")
    y, z = f // nz, f % nz
    n_f = 2 * nz
    partner = (1 - y) * nz + z
    rows, feats = 128, 512
    peers = ORDER

    def zdev(k):
        return {"rep": r, "fsdp": y * nz + (z + k) % nz}

    barrier = pltpu.get_barrier_semaphore()

    def greet_f(k, c):
        pl.semaphore_signal(barrier, inc=1, device_id={"rep": r, "fsdp": (f + k) % n_f}, device_id_type=MESH)
        return c

    def greet_r(k, c):
        pl.semaphore_signal(barrier, inc=1, device_id={"rep": (r + k) % n_rep, "fsdp": f}, device_id_type=MESH)
        return c

    lax.fori_loop(1, n_f, greet_f, 0)
    lax.fori_loop(1, n_rep, greet_r, 0)

    local = [
        pltpu.make_async_copy(tok_hbm, x, loc.at[0]),
        pltpu.make_async_copy(w_hbm, wcat.at[pl.ds(feats, feats), :], loc.at[1]),
        pltpu.make_async_copy(u_hbm, ucat.at[0], loc.at[2]),
        pltpu.make_async_copy(fm_hbm, fm, loc.at[3]),
        pltpu.make_async_copy(sm_hbm, sm, loc.at[4]),
    ]
    for c in local:
        c.start()

    frag = frag_ref[0]
    local[1].wait()
    sel = wcat[pl.ds(feats, feats), 0:128]
    for j in range(1, 4):
        sel = jnp.where(frag == j, wcat[pl.ds(feats, feats), j * 128 : (j + 1) * 128], sel)
    wsel[...] = sel.reshape(wsel.shape)

    local[0].wait()

    def squares(i, acc):
        for j in range(4):
            v = x[:, pl.ds(pl.multiple_of(i * 512 + j * 128, 128), 128)].astype(jnp.float32)
            acc = acc + v * v
        return acc

    acc = lax.fori_loop(0, 16, squares, jnp.zeros((rows, 128), jnp.float32))
    mean = jnp.sum(acc, axis=1, keepdims=True) / (16 * feats)
    scale_ref[...] = jnp.broadcast_to(lax.rsqrt(mean + 1e-05), (rows, 128))
    local[2].wait()
    for j in range(4):
        cols = slice(j * 128, (j + 1) * 128)
        ucat[0, :, cols] = (ucat[0, :, cols].astype(jnp.float32) * scale_ref[...]).astype(jnp.bfloat16)

    pl.semaphore_wait(barrier, n_f - 1 + n_rep - 1)

    w_copy = pltpu.make_async_remote_copy(
        src_ref=wcat.at[pl.ds(feats, feats), :],
        dst_ref=wcat.at[pl.ds(0, feats), :],
        send_sem=one_s.at[0],
        recv_sem=one_r.at[0],
        device_id={"rep": r, "fsdp": partner},
        device_id_type=MESH,
    )

    def send_rows(k, c):
        dst = (r + k) % n_rep
        pltpu.make_async_remote_copy(
            src_ref=wsel.at[dst],
            dst_ref=wrecv.at[k - 1],
            send_sem=one_s.at[1],
            recv_sem=one_r.at[1],
            device_id={"rep": dst, "fsdp": f},
            device_id_type=MESH,
        ).start()
        return c

    u_copies, p_copies, o_copies, v_copies = [], [], [], []
    for i, k in enumerate(peers):
        u_copies.append(
            pltpu.make_async_remote_copy(
                src_ref=ucat.at[0], dst_ref=ucat.at[i + 1], send_sem=u_s.at[i], recv_sem=u_r.at[i], device_id=zdev(k), device_id_type=MESH
            )
        )
        zk = (z + k) % nz
        for kind, dst, yk in ((0, tp, 1 - y), (1, to, y)):
            col = pl.multiple_of((yk * nz + zk) * feats, feats)
            (o_copies if kind else p_copies).append(
                pltpu.make_async_remote_copy(
                    src_ref=tok_hbm.at[:, pl.ds(col, feats)],
                    dst_ref=dst.at[i + 1],
                    send_sem=t_s.at[kind * 7 + i],
                    recv_sem=t_r.at[kind * 7 + i],
                    device_id=zdev(k),
                    device_id_type=MESH,
                )
            )
        v_copies.append(
            pltpu.make_async_remote_copy(
                src_ref=vsend.at[i], dst_ref=vrecv.at[i], send_sem=v_s.at[i], recv_sem=v_r.at[i], device_id=zdev(nz - k), device_id_type=MESH
            )
        )
    for c in u_copies:
        c.start()
    for c in p_copies[:4]:
        c.start()
    w_copy.start()
    lax.fori_loop(1, n_rep, send_rows, 0)
    for c in p_copies[4:]:
        c.start()
    for c in o_copies:
        c.start()

    def gained(src, i, kind, yk):
        first = (yk * nz + z) * 4
        at = pl.ds(pl.multiple_of(i * rows, rows), rows)
        for j in range(4):
            g = gain_ref[pl.ds(first + j, 1), :]
            v = src(j).astype(jnp.float32) * g
            tg[at, kind * feats + j * 128 : kind * feats + (j + 1) * 128] = v.astype(jnp.bfloat16)

    def own(yk):
        return lambda j: x[:, pl.ds(pl.multiple_of((yk * nz + z) * feats + j * 128, 128), 128)]

    def block(ref, i):
        return lambda j: ref[i, :, j * 128 : (j + 1) * 128]

    gained(own(1 - y), 0, 0, 1 - y)
    gained(own(y), 0, 1, y)

    pltpu.make_async_copy(wrecv, wrecv, one_r.at[1]).wait()

    def add_rows(k, acc):
        return acc + wrecv[k].astype(jnp.float32)

    total_rows = lax.fori_loop(0, n_rep - 1, add_rows, wsel[r].astype(jnp.float32))
    share_g, share_u = gp_ref[0, 0], mom_ref[0, 0]
    for j in range(1, 4):
        share_g = jnp.where(frag == j, gp_ref[j, 0], share_g)
        share_u = jnp.where(frag == j, mom_ref[j, 0], share_u)
    delta = share_g - total_rows / n_rep
    u_new = outer_mom * share_u + delta
    g_new = share_g - outer_rate * (outer_mom * u_new + delta)
    gnew[...] = g_new
    for j in range(4):
        ng_ref[j, 0] = jnp.where(frag == j, g_new, gp_ref[j, 0])
        nm_ref[j, 0] = jnp.where(frag == j, u_new, mom_ref[j, 0])

    def send_new(k, c):
        pltpu.make_async_remote_copy(
            src_ref=gnew,
            dst_ref=grow.at[k - 1],
            send_sem=one_s.at[2],
            recv_sem=one_r.at[2],
            device_id={"rep": (r + k) % n_rep, "fsdp": f},
            device_id_type=MESH,
        ).start()
        return c

    lax.fori_loop(1, n_rep, send_new, 0)

    for i in range(7):
        p_copies[i].wait_recv()
        gained(block(tp, i + 1), i + 1, 0, 1 - y)
    for c in u_copies:
        c.wait_recv()

    def grad(kind, m):
        cols = slice(kind * feats + m * 256, kind * feats + (m + 1) * 256)
        return lax.dot_general(
            tg[:, cols], ucat[...].reshape(nz * rows, feats), (((0,), (0,)), ((), ())), preferred_element_type=jnp.float32
        )

    for m in range(2):
        gsend[m * 256 : (m + 1) * 256, :] = grad(0, m).astype(jnp.bfloat16)
    g_copy = pltpu.make_async_remote_copy(
        src_ref=gsend,
        dst_ref=grecv,
        send_sem=one_s.at[3],
        recv_sem=one_r.at[3],
        device_id={"rep": r, "fsdp": partner},
        device_id_type=MESH,
    )
    g_copy.start()

    w_copy.wait_recv()
    vown[...] = jnp.dot(tg[0:rows, :], wcat[...], preferred_element_type=jnp.float32)

    pltpu.make_async_copy(grow, grow, one_r.at[2]).wait()
    gfull[r] = gnew[...]

    def place(k, c):
        gfull[(r + n_rep - k) % n_rep] = grow[k - 1]
        return c

    lax.fori_loop(1, n_rep, place, 0)

    for i in range(7):
        o_copies[i].wait_recv()
        gained(block(to, i + 1), i + 1, 1, y)
        at = slice((i + 1) * rows, (i + 2) * rows)
        vsend[i] = jnp.dot(tg[at, :], wcat[...], preferred_element_type=jnp.float32).astype(jnp.bfloat16)
        v_copies[i].start()

    g_copy.wait_recv()
    acc = jnp.zeros((8, feats), jnp.float32)
    for m in range(2):
        at = slice(m * 256, (m + 1) * 256)
        g = grad(1, m) + grecv[at, :].astype(jnp.float32)
        gown[at, :] = g
        acc = acc + jnp.sum((g * g).reshape(32, 8, feats), axis=0)
    nsend[...] = acc[:, 0:128] + acc[:, 128:256] + acc[:, 256:384] + acc[:, 384:512]

    def send_norm(k, c):
        pltpu.make_async_remote_copy(
            src_ref=nsend,
            dst_ref=nrecv.at[k - 1],
            send_sem=one_s.at[4],
            recv_sem=one_r.at[4],
            device_id={"rep": r, "fsdp": (f + k) % n_f},
            device_id_type=MESH,
        ).start()
        return c

    lax.fori_loop(1, n_f, send_norm, 0)
    local[3].wait()
    local[4].wait()
    pltpu.make_async_copy(nrecv, nrecv, one_r.at[4]).wait()
    tile = nsend[...] + jnp.sum(nrecv[...], axis=0)
    total = jnp.sum(jnp.sum(tile, axis=1, keepdims=True), axis=0, keepdims=True)
    factor = jnp.minimum(1.0, clip_bound / (jnp.sqrt(total) + 1e-06))

    def update(i, c):
        at = pl.ds(pl.multiple_of(i * 64, 64), 64)
        wat = pl.ds(pl.multiple_of(feats + i * 64, 64), 64)
        rows_new = gfull[pl.ds(i * 4, 4)].reshape(64, 128)
        for j in range(4):
            cols = slice(j * 128, (j + 1) * 128)
            clipped = gown[at, cols] * factor
            moment = 0.9 * fm[at, cols].astype(jnp.float32) + 0.1 * clipped
            square = 0.95 * sm[at, cols].astype(jnp.float32) + 0.05 * clipped * clipped
            wf = wcat[wat, cols].astype(jnp.float32)
            inner = wf - inner_rate * (moment / (jnp.sqrt(square) + 1e-08) + decay_rate * wf)
            merged = blend * inner + (1.0 - blend) * rows_new
            nw[at, cols] = jnp.where(frag == j, merged, inner).astype(jnp.bfloat16)
        return c

    lax.fori_loop(0, 8, update, 0)
    nw_copy = pltpu.make_async_copy(nw, nw_hbm, loc.at[5])
    nw_copy.start()

    for c in v_copies:
        c.wait_recv()
    for j in range(4):
        cols = slice(j * 128, (j + 1) * 128)
        acc = vown[:, cols]
        for i in range(7):
            acc = acc + vrecv[i, :, cols].astype(jnp.float32)
        vout[:, cols] = (acc * scale_ref[...]).astype(jnp.bfloat16)
    v_out = pltpu.make_async_copy(vout, val_hbm, loc.at[6])
    v_out.start()

    for c in u_copies + p_copies + o_copies + v_copies + [w_copy, g_copy]:
        c.wait_send()
    pltpu.make_async_copy(wrecv, wrecv, one_s.at[1]).wait()
    pltpu.make_async_copy(grow, grow, one_s.at[2]).wait()
    pltpu.make_async_copy(nrecv, nrecv, one_s.at[4]).wait()
    nw_copy.wait()
    v_out.wait()


def per_device(n_rep, n_fsdp, tokens, norm_gain, weights, first_moment, second_moment, upstream, global_params, outer_momentum, fragment):
    nz = n_fsdp // 2
    bf, f32 = jnp.bfloat16, jnp.float32
    vm, anywhere = pl.BlockSpec(memory_space=pltpu.VMEM), pl.BlockSpec(memory_space=pl.ANY)
    dma = pltpu.SemaphoreType.DMA
    out = pl.pallas_call(
        functools.partial(kernel, n_rep, nz),
        out_shape=(
            jax.ShapeDtypeStruct((512, 512), bf),
            jax.ShapeDtypeStruct((128, 512), bf),
            jax.ShapeDtypeStruct(global_params.shape, f32),
            jax.ShapeDtypeStruct(outer_momentum.shape, f32),
        ),
        in_specs=[anywhere, vm, anywhere, anywhere, anywhere, anywhere, vm, vm, pl.BlockSpec(memory_space=pltpu.SMEM)],
        out_specs=(anywhere, anywhere, vm, vm),
        scratch_shapes=[
            pltpu.VMEM((128, 8192), bf),
            pltpu.VMEM((8, 128, 512), bf),
            pltpu.VMEM((8, 128, 512), bf),
            pltpu.VMEM((1024, 1024), bf),
            pltpu.VMEM((1024, 512), bf),
            pltpu.VMEM((8, 128, 512), bf),
            pltpu.VMEM((512, 512), bf),
            pltpu.VMEM((512, 512), bf),
            pltpu.VMEM((512, 512), bf),
            pltpu.VMEM((512, 512), f32),
            pltpu.VMEM((512, 512), bf),
            pltpu.VMEM((512, 512), bf),
            pltpu.VMEM((7, 128, 512), bf),
            pltpu.VMEM((7, 128, 512), bf),
            pltpu.VMEM((128, 512), f32),
            pltpu.VMEM((128, 512), bf),
            pltpu.VMEM((128, 128), f32),
            pltpu.VMEM((n_rep, 16, 128), bf),
            pltpu.VMEM((n_rep - 1, 16, 128), bf),
            pltpu.VMEM((16, 128), f32),
            pltpu.VMEM((n_rep - 1, 16, 128), f32),
            pltpu.VMEM((n_rep, 16, 128), f32),
            pltpu.VMEM((8, 128), f32),
            pltpu.VMEM((n_fsdp - 1, 8, 128), f32),
            dma((7,)),
            dma((14,)),
            dma((14,)),
            dma((7,)),
            dma((7,)),
            dma((7,)),
            dma((7,)),
            dma((5,)),
            dma((5,)),
        ],
        compiler_params=pltpu.CompilerParams(collective_id=0, has_side_effects=True, vmem_limit_bytes=60 * 1024 * 1024),
        name="step",
    )(
        tokens[0],
        norm_gain.reshape(64, 128),
        weights[0],
        first_moment[0],
        second_moment[0],
        upstream[0],
        global_params,
        outer_momentum,
        fragment,
    )
    return (out[0][None], out[1][None], out[2], out[3])


def solution(mesh):
    placed = (
        P("rep", "fsdp", None),
        P(),
        P("rep", "fsdp", None),
        P("rep", "fsdp", None),
        P("rep", "fsdp", None),
        P("rep", "fsdp", None),
        P(None, "fsdp", "rep", None),
        P(None, "fsdp", "rep", None),
        P(),
    )
    return jax.shard_map(
        functools.partial(per_device, mesh.shape["rep"], mesh.shape["fsdp"]),
        mesh=mesh,
        in_specs=placed,
        out_specs=(
            P("rep", "fsdp", None),
            P("rep", "fsdp", None),
            P(None, "fsdp", "rep", None),
            P(None, "fsdp", "rep", None),
        ),
        check_vma=False,
    )
```

```python
import functools

import jax
import jax.numpy as jnp
from jax import lax
from jax.experimental import pallas as pl
from jax.experimental.pallas import tpu as pltpu
from jax.sharding import PartitionSpec as P

MESH = pl.DeviceIdType.MESH

clip_bound = 1.0
inner_rate = 0.02
decay_rate = 0.1
outer_rate = 0.7
outer_mom = 0.9
blend = 0.5

ORDER = (1, 7, 2, 6, 3, 5, 4)
AHEAD, BACK = (0, 1, 3, 5, 7), (0, 2, 4, 6, 7)
FAR = (7, 5, 6, 3, 4, 1, 2)


def kernel(
    n_rep,
    nz,
    tok_hbm,
    gain_ref,
    w_hbm,
    fm_hbm,
    sm_hbm,
    u_hbm,
    gp_ref,
    mom_ref,
    frag_ref,
    nw_hbm,
    val_hbm,
    ng_ref,
    nm_ref,
    x,
    xn,
    tp,
    to,
    w,
    wp,
    u,
    fm,
    sm,
    nw,
    gown,
    gsend,
    grecv,
    vsend,
    vrecv,
    vown,
    vout,
    scale_ref,
    wsel,
    wrecv,
    gnew,
    grow,
    gfull,
    nsend,
    nrecv,
    loc,
    t_s,
    t_r,
    u_s,
    u_r,
    v_s,
    v_r,
    one_s,
    one_r,
):
    r = lax.axis_index("rep")
    f = lax.axis_index("fsdp")
    y, z = f // nz, f % nz
    n_f = 2 * nz
    rows, feats = 128, 512
    f32, bf16 = jnp.float32, jnp.bfloat16

    def zdev(k):
        return {"rep": r, "fsdp": y * nz + (z + k) % nz}

    partner = {"rep": r, "fsdp": (1 - y) * nz + z}

    def remote(src, dst, send_sem, recv_sem, device):
        return pltpu.make_async_remote_copy(
            src_ref=src, dst_ref=dst, send_sem=send_sem, recv_sem=recv_sem, device_id=device, device_id_type=MESH
        )

    barrier = pltpu.get_barrier_semaphore()

    def greet_f(k, c):
        pl.semaphore_signal(barrier, inc=1, device_id={"rep": r, "fsdp": (f + k) % n_f}, device_id_type=MESH)
        return c

    def greet_r(k, c):
        pl.semaphore_signal(barrier, inc=1, device_id={"rep": (r + k) % n_rep, "fsdp": f}, device_id_type=MESH)
        return c

    local = [
        pltpu.make_async_copy(tok_hbm, x, loc.at[0]),
        pltpu.make_async_copy(w_hbm, w, loc.at[1]),
        pltpu.make_async_copy(u_hbm, u.at[0], loc.at[2]),
        pltpu.make_async_copy(fm_hbm, fm, loc.at[3]),
        pltpu.make_async_copy(sm_hbm, sm, loc.at[4]),
    ]
    for c in local:
        c.start()
    lax.fori_loop(1, n_f, greet_f, 0)
    lax.fori_loop(1, n_rep, greet_r, 0)

    frag = frag_ref[0]
    local[0].wait()

    def squares(i, acc):
        for j in range(4):
            v = x[:, pl.ds(pl.multiple_of(i * 512 + j * 128, 128), 128)].astype(f32)
            acc = acc + v * v
        return acc

    acc = lax.fori_loop(0, 2 * nz, squares, jnp.zeros((rows, 128), f32))
    mean = jnp.sum(acc, axis=1, keepdims=True) / (2 * nz * feats)
    scale_ref[...] = jnp.broadcast_to(lax.rsqrt(mean + 1e-05), (rows, 128))

    def normed(block, dst):
        for j in range(4):
            g = gain_ref[pl.ds(block * 4 + j, 1), :]
            v = x[:, pl.ds(pl.multiple_of(block * feats + j * 128, 128), 128)].astype(f32)
            dst[:, j * 128 : (j + 1) * 128] = (v * scale_ref[...] * g).astype(bf16)

    copies = []

    def keep(c):
        c.start()
        copies.append(c)
        return c

    t_in = {}

    def prepare(kind, i):
        block = (1 - y if kind == 0 else y) * nz + (z + ORDER[i - 1]) % nz
        normed(block, xn.at[kind * 7 + i - 1])

    def send_tokens(kind, i):
        n = kind * 7 + i - 1
        t_in[kind, i] = keep(remote(xn.at[n], (to if kind else tp).at[i], t_s.at[n], t_r.at[n], zdev(ORDER[i - 1])))

    for i in FAR[:3]:
        prepare(0, i)
    local[1].wait()
    sel = w[:, 0:128]
    for j in range(1, 4):
        sel = jnp.where(frag == j, w[:, j * 128 : (j + 1) * 128], sel)
    wsel[...] = sel.reshape(wsel.shape)
    local[2].wait()

    pl.semaphore_wait(barrier, n_f - 1 + n_rep - 1)

    def hop(h):
        part = [slice(0, rows), slice(0, rows)] if h < 4 else [slice(0, rows // 2), slice(rows // 2, rows)]
        return [
            keep(remote(u.at[s[h - 1], p], u.at[s[h], p], u_s.at[2 * h - 2 + n], u_r.at[2 * h - 2 + n], zdev((1, nz - 1)[n])))
            for n, (s, p) in enumerate(zip((AHEAD, BACK), part))
        ]

    u_in = hop(1)
    for i in FAR[:3]:
        send_tokens(0, i)
    w_copy = keep(remote(w, wp, one_s.at[0], one_r.at[0], partner))

    def send_rows(k, c):
        dst = (r + k) % n_rep
        remote(wsel.at[dst], wrecv.at[k - 1], one_s.at[1], one_r.at[1], {"rep": dst, "fsdp": f}).start()
        return c

    lax.fori_loop(1, n_rep, send_rows, 0)
    for i in FAR[3:]:
        prepare(0, i)

    for c in u_in:
        c.wait_recv()
    u_in = hop(2)
    for i in FAR[3:5]:
        send_tokens(0, i)
    normed((1 - y) * nz + z, tp.at[0])
    normed(y * nz + z, to.at[0])
    for c in u_in:
        c.wait_recv()
    u_in = hop(3)
    for i in FAR[5:]:
        send_tokens(0, i)
    for i in FAR:
        prepare(1, i)

    pltpu.make_async_copy(wrecv, wrecv, one_r.at[1]).wait()

    def add_rows(k, acc):
        return acc + wrecv[k].astype(f32)

    total_rows = lax.fori_loop(0, n_rep - 1, add_rows, wsel[r].astype(f32))
    share_g, share_u = gp_ref[0, 0], mom_ref[0, 0]
    for j in range(1, 4):
        share_g = jnp.where(frag == j, gp_ref[j, 0], share_g)
        share_u = jnp.where(frag == j, mom_ref[j, 0], share_u)
    delta = share_g - total_rows / n_rep
    u_new = outer_mom * share_u + delta
    g_new = share_g - outer_rate * (outer_mom * u_new + delta)
    gnew[...] = g_new

    def send_new(k, c):
        remote(gnew, grow.at[k - 1], one_s.at[2], one_r.at[2], {"rep": (r + k) % n_rep, "fsdp": f}).start()
        return c

    for c in u_in:
        c.wait_recv()
    u_in = hop(4)
    for i in FAR:
        send_tokens(1, i)
    lax.fori_loop(1, n_rep, send_new, 0)
    for j in range(4):
        ng_ref[j, 0] = jnp.where(frag == j, g_new, gp_ref[j, 0])
        nm_ref[j, 0] = jnp.where(frag == j, u_new, mom_ref[j, 0])

    def grad(t, first, count, cols):
        k = count * rows
        return lax.dot_general(
            t[first : first + count, :, cols].reshape(k, -1),
            u[first : first + count].reshape(k, feats),
            (((0,), (0,)), ((), ())),
            preferred_element_type=f32,
        )

    for i in FAR:
        t_in[0, i].wait_recv()
    for c in u_in:
        c.wait_recv()
    halves = (slice(0, 256), slice(256, 512))
    for m in halves:
        gsend[m, :] = grad(tp, 0, nz, m).astype(bf16)
    g_copy = keep(remote(gsend, grecv, one_s.at[3], one_r.at[3], partner))

    w_copy.wait_recv()

    def partial(i):
        return jnp.dot(tp[i], wp[...], preferred_element_type=f32) + jnp.dot(to[i], w[...], preferred_element_type=f32)

    vown[...] = partial(0)

    t_in[1, 7].wait_recv()
    vsend[0] = partial(7).astype(bf16)
    first_half, last_half = slice(0, rows // 2), slice(rows // 2, rows)
    v_in = [
        keep(remote(vsend.at[0, p], vrecv.at[0, p], v_s.at[n], v_r.at[n], zdev((1, nz - 1)[n])))
        for n, p in enumerate((first_half, last_half))
    ]
    for m in halves:
        gown[m, :] = grad(to, 0, 1, m) + grad(to, 7, 1, m)

    pltpu.make_async_copy(grow, grow, one_r.at[2]).wait()
    gfull[r] = gnew[...]

    def place(k, c):
        gfull[(r + n_rep - k) % n_rep] = grow[k - 1]
        return c

    lax.fori_loop(1, n_rep, place, 0)

    for s in (2, 3):
        a, b = {2: (6, 5), 3: (4, 3)}[s]
        at = 2 * s - 2
        t_in[1, a].wait_recv()
        ahead = partial(a)
        t_in[1, b].wait_recv()
        back = partial(b)
        v_in[0].wait_recv()
        if s == 2:
            vsend[at, first_half] = (ahead[first_half] + vrecv[0, first_half].astype(f32)).astype(bf16)
            vsend[at, last_half] = ahead[last_half].astype(bf16)
        else:
            vsend[at] = (ahead + vrecv[at - 2].astype(f32)).astype(bf16)
        ahead_copy = keep(remote(vsend.at[at], vrecv.at[at], v_s.at[at], v_r.at[at], zdev(1)))
        v_in[1].wait_recv()
        if s == 2:
            vsend[at + 1, last_half] = (back[last_half] + vrecv[0, last_half].astype(f32)).astype(bf16)
            vsend[at + 1, first_half] = back[first_half].astype(bf16)
        else:
            vsend[at + 1] = (back + vrecv[at - 1].astype(f32)).astype(bf16)
        back_copy = keep(remote(vsend.at[at + 1], vrecv.at[at + 1], v_s.at[at + 1], v_r.at[at + 1], zdev(nz - 1)))
        v_in = [ahead_copy, back_copy]
        for m in halves:
            gown[m, :] += grad(to, b, 2, m)

    g_copy.wait_recv()
    t_in[1, 1].wait_recv()
    t_in[1, 2].wait_recv()
    acc = jnp.zeros((8, feats), f32)
    for m in halves:
        g = gown[m, :] + grecv[m, :].astype(f32) + grad(to, 1, 2, m)
        gown[m, :] = g
        acc = acc + jnp.sum((g * g).reshape(32, 8, feats), axis=0)
    nsend[...] = acc[:, 0:128] + acc[:, 128:256] + acc[:, 256:384] + acc[:, 384:512]

    def send_norm(k, c):
        remote(nsend, nrecv.at[k - 1], one_s.at[4], one_r.at[4], {"rep": r, "fsdp": (f + k) % n_f}).start()
        return c

    lax.fori_loop(1, n_f, send_norm, 0)

    ahead, back = partial(2), partial(1)
    v_in[0].wait_recv()
    vsend[6] = (ahead + vrecv[4].astype(f32)).astype(bf16)
    ahead_copy = keep(remote(vsend.at[6], vrecv.at[6], v_s.at[6], v_r.at[6], zdev(1)))
    v_in[1].wait_recv()
    vsend[7] = (back + vrecv[5].astype(f32)).astype(bf16)
    back_copy = keep(remote(vsend.at[7], vrecv.at[7], v_s.at[7], v_r.at[7], zdev(nz - 1)))

    local[3].wait()
    local[4].wait()
    pltpu.make_async_copy(nrecv, nrecv, one_r.at[4]).wait()
    tile = nsend[...] + jnp.sum(nrecv[...], axis=0)
    total = jnp.sum(jnp.sum(tile, axis=1, keepdims=True), axis=0, keepdims=True)
    factor = jnp.minimum(1.0, clip_bound / (jnp.sqrt(total) + 1e-06))

    def update(i, c):
        at = pl.ds(pl.multiple_of(i * 64, 64), 64)
        rows_new = gfull[pl.ds(i * 4, 4)].reshape(64, 128)
        for j in range(4):
            cols = slice(j * 128, (j + 1) * 128)
            clipped = gown[at, cols] * factor
            moment = 0.9 * fm[at, cols].astype(f32) + 0.1 * clipped
            square = 0.95 * sm[at, cols].astype(f32) + 0.05 * clipped * clipped
            wf = w[at, cols].astype(f32)
            inner = wf - inner_rate * (moment / (jnp.sqrt(square) + 1e-08) + decay_rate * wf)
            merged = blend * inner + (1.0 - blend) * rows_new
            nw[at, cols] = jnp.where(frag == j, merged, inner).astype(bf16)
        return c

    lax.fori_loop(0, 8, update, 0)
    nw_copy = pltpu.make_async_copy(nw, nw_hbm, loc.at[5])
    nw_copy.start()

    ahead_copy.wait_recv()
    back_copy.wait_recv()
    vout[...] = (vown[...] + vrecv[6].astype(f32) + vrecv[7].astype(f32)).astype(bf16)
    v_out = pltpu.make_async_copy(vout, val_hbm, loc.at[6])
    v_out.start()

    for c in copies:
        c.wait_send()
    pltpu.make_async_copy(wrecv, wrecv, one_s.at[1]).wait()
    pltpu.make_async_copy(grow, grow, one_s.at[2]).wait()
    pltpu.make_async_copy(nrecv, nrecv, one_s.at[4]).wait()
    nw_copy.wait()
    v_out.wait()


def hand_over(*refs):
    n = len(refs) // 2
    sems = refs[-1]
    copies = [pltpu.make_async_copy(refs[i], refs[n + i], sems.at[i]) for i in range(n)]
    for c in copies:
        c.start()
    for c in copies:
        c.wait()


def per_device(n_rep, n_fsdp, tokens, norm_gain, weights, first_moment, second_moment, upstream, global_params, outer_momentum, fragment):
    nz = n_fsdp // 2
    bf, f32 = jnp.bfloat16, jnp.float32
    vm, anywhere = pl.BlockSpec(memory_space=pltpu.VMEM), pl.BlockSpec(memory_space=pl.ANY)
    dma = pltpu.SemaphoreType.DMA
    out = pl.pallas_call(
        functools.partial(kernel, n_rep, nz),
        out_shape=(
            jax.ShapeDtypeStruct((512, 512), bf),
            jax.ShapeDtypeStruct((128, 512), bf),
            jax.ShapeDtypeStruct(global_params.shape, f32),
            jax.ShapeDtypeStruct(outer_momentum.shape, f32),
        ),
        in_specs=[anywhere, vm, anywhere, anywhere, anywhere, anywhere, vm, vm, pl.BlockSpec(memory_space=pltpu.SMEM)],
        out_specs=(anywhere, anywhere, vm, vm),
        scratch_shapes=[
            pltpu.VMEM((128, 8192), bf),
            pltpu.VMEM((14, 128, 512), bf),
            pltpu.VMEM((8, 128, 512), bf),
            pltpu.VMEM((8, 128, 512), bf),
            pltpu.VMEM((512, 512), bf),
            pltpu.VMEM((512, 512), bf),
            pltpu.VMEM((8, 128, 512), bf),
            pltpu.VMEM((512, 512), bf),
            pltpu.VMEM((512, 512), bf),
            pltpu.VMEM((512, 512), bf),
            pltpu.VMEM((512, 512), f32),
            pltpu.VMEM((512, 512), bf),
            pltpu.VMEM((512, 512), bf),
            pltpu.VMEM((8, 128, 512), bf),
            pltpu.VMEM((8, 128, 512), bf),
            pltpu.VMEM((128, 512), f32),
            pltpu.VMEM((128, 512), bf),
            pltpu.VMEM((128, 128), f32),
            pltpu.VMEM((n_rep, 16, 128), bf),
            pltpu.VMEM((n_rep - 1, 16, 128), bf),
            pltpu.VMEM((16, 128), f32),
            pltpu.VMEM((n_rep - 1, 16, 128), f32),
            pltpu.VMEM((n_rep, 16, 128), f32),
            pltpu.VMEM((8, 128), f32),
            pltpu.VMEM((n_fsdp - 1, 8, 128), f32),
            dma((7,)),
            dma((14,)),
            dma((14,)),
            dma((8,)),
            dma((8,)),
            dma((8,)),
            dma((8,)),
            dma((5,)),
            dma((5,)),
        ],
        compiler_params=pltpu.CompilerParams(collective_id=0, has_side_effects=True, vmem_limit_bytes=60 * 1024 * 1024),
        name="step",
    )(
        tokens[0],
        norm_gain.reshape(64, 128),
        weights[0],
        first_moment[0],
        second_moment[0],
        upstream[0],
        global_params,
        outer_momentum,
        fragment,
    )
    out = pl.pallas_call(
        hand_over,
        out_shape=tuple(jax.ShapeDtypeStruct(o.shape, o.dtype) for o in out),
        in_specs=[anywhere] * 4,
        out_specs=(anywhere,) * 4,
        scratch_shapes=[dma((4,))],
        compiler_params=pltpu.CompilerParams(vmem_limit_bytes=60 * 1024 * 1024),
        name="hand_over",
    )(*out)
    return (out[0][None], out[1][None], out[2], out[3])


def solution(mesh):
    placed = (
        P("rep", "fsdp", None),
        P(),
        P("rep", "fsdp", None),
        P("rep", "fsdp", None),
        P("rep", "fsdp", None),
        P("rep", "fsdp", None),
        P(None, "fsdp", "rep", None),
        P(None, "fsdp", "rep", None),
        P(),
    )
    return jax.shard_map(
        functools.partial(per_device, mesh.shape["rep"], mesh.shape["fsdp"]),
        mesh=mesh,
        in_specs=placed,
        out_specs=(
            P("rep", "fsdp", None),
            P("rep", "fsdp", None),
            P(None, "fsdp", "rep", None),
            P(None, "fsdp", "rep", None),
        ),
        check_vma=False,
    )
```

```python
import functools

import jax
import jax.numpy as jnp
from jax import lax
from jax.experimental import pallas as pl
from jax.experimental.pallas import tpu as pltpu
from jax.sharding import PartitionSpec as P

MESH = pl.DeviceIdType.MESH

clip_bound = 1.0
inner_rate = 0.02
decay_rate = 0.1
outer_rate = 0.7
outer_mom = 0.9
blend = 0.5

ORDER = (1, 7, 2, 6, 3, 5, 4)
AHEAD, BACK = (0, 1, 3, 5, 7), (0, 2, 4, 6, 7)
FAR = (7, 5, 6, 3, 4, 1, 2)


def kernel(
    n_rep,
    nz,
    tok_hbm,
    gain_hbm,
    w_hbm,
    fm_hbm,
    sm_hbm,
    u_hbm,
    gp_hbm,
    mom_hbm,
    frag_ref,
    nw,
    val,
    ng_ref,
    nm_ref,
    x,
    xn,
    tp,
    to,
    w,
    wp,
    u,
    fm,
    sm,
    gain_ref,
    gp_ref,
    mom_ref,
    gown,
    gsend,
    grecv,
    vsend,
    vrecv,
    vown,
    scale_ref,
    wsel,
    wrecv,
    gnew,
    grow,
    gfull,
    nsend,
    nrecv,
    loc,
    t_s,
    t_r,
    u_s,
    u_r,
    v_s,
    v_r,
    one_s,
    one_r,
):
    r = lax.axis_index("rep")
    f = lax.axis_index("fsdp")
    y, z = f // nz, f % nz
    n_f = 2 * nz
    rows, feats = 128, 512
    f32, bf16 = jnp.float32, jnp.bfloat16

    def zdev(k):
        return {"rep": r, "fsdp": y * nz + (z + k) % nz}

    partner = {"rep": r, "fsdp": (1 - y) * nz + z}

    def remote(src, dst, send_sem, recv_sem, device):
        return pltpu.make_async_remote_copy(
            src_ref=src, dst_ref=dst, send_sem=send_sem, recv_sem=recv_sem, device_id=device, device_id_type=MESH
        )

    barrier = pltpu.get_barrier_semaphore()

    def greet_f(k, c):
        pl.semaphore_signal(barrier, inc=1, device_id={"rep": r, "fsdp": (f + k) % n_f}, device_id_type=MESH)
        return c

    def greet_r(k, c):
        pl.semaphore_signal(barrier, inc=1, device_id={"rep": (r + k) % n_rep, "fsdp": f}, device_id_type=MESH)
        return c

    local = [
        pltpu.make_async_copy(src, dst, loc.at[n])
        for n, (src, dst) in enumerate(
            (
                (u_hbm, u.at[0]),
                (w_hbm, w),
                (tok_hbm, x),
                (gain_hbm, gain_ref),
                (gp_hbm, gp_ref),
                (mom_hbm, mom_ref),
                (fm_hbm, fm),
                (sm_hbm, sm),
            )
        )
    ]
    for c in local:
        c.start()
    lax.fori_loop(1, n_f, greet_f, 0)
    lax.fori_loop(1, n_rep, greet_r, 0)

    copies = []

    def keep(c):
        c.start()
        copies.append(c)
        return c

    def hop(h):
        part = [slice(0, rows), slice(0, rows)] if h < 4 else [slice(0, rows // 2), slice(rows // 2, rows)]
        return [
            keep(remote(u.at[s[h - 1], p], u.at[s[h], p], u_s.at[2 * h - 2 + n], u_r.at[2 * h - 2 + n], zdev((1, nz - 1)[n])))
            for n, (s, p) in enumerate(zip((AHEAD, BACK), part))
        ]

    local[0].wait()
    pl.semaphore_wait(barrier, n_f - 1 + n_rep - 1)
    u_in = hop(1)
    local[1].wait()
    w_copy = keep(remote(w, wp, one_s.at[0], one_r.at[0], partner))
    local[2].wait()

    def squares(i, acc):
        for j in range(4):
            v = x[:, pl.ds(pl.multiple_of(i * 512 + j * 128, 128), 128)].astype(f32)
            acc = acc + v * v
        return acc

    acc = lax.fori_loop(0, 2 * nz, squares, jnp.zeros((rows, 128), f32))
    mean = jnp.sum(acc, axis=1, keepdims=True) / (2 * nz * feats)
    scale_ref[...] = jnp.broadcast_to(lax.rsqrt(mean + 1e-05), (rows, 128))

    def normed(block, dst):
        for j in range(4):
            g = gain_ref[pl.ds(block * 4 + j, 1), :]
            v = x[:, pl.ds(pl.multiple_of(block * feats + j * 128, 128), 128)].astype(f32)
            dst[:, j * 128 : (j + 1) * 128] = (v * scale_ref[...] * g).astype(bf16)

    t_in = {}

    def prepare(kind, i):
        block = (1 - y if kind == 0 else y) * nz + (z + ORDER[i - 1]) % nz
        normed(block, xn.at[kind * 7 + i - 1])

    def send_tokens(kind, i):
        n = kind * 7 + i - 1
        t_in[kind, i] = keep(remote(xn.at[n], (to if kind else tp).at[i], t_s.at[n], t_r.at[n], zdev(ORDER[i - 1])))

    local[3].wait()
    for i in FAR[:3]:
        prepare(0, i)
        send_tokens(0, i)
    frag = frag_ref[0]
    sel = w[:, 0:128]
    for j in range(1, 4):
        sel = jnp.where(frag == j, w[:, j * 128 : (j + 1) * 128], sel)
    wsel[...] = sel.reshape(wsel.shape)

    def send_rows(k, c):
        dst = (r + k) % n_rep
        remote(wsel.at[dst], wrecv.at[k - 1], one_s.at[1], one_r.at[1], {"rep": dst, "fsdp": f}).start()
        return c

    lax.fori_loop(1, n_rep, send_rows, 0)
    for i in FAR[3:]:
        prepare(0, i)

    for c in u_in:
        c.wait_recv()
    u_in = hop(2)
    for i in FAR[3:5]:
        send_tokens(0, i)
    normed((1 - y) * nz + z, tp.at[0])
    normed(y * nz + z, to.at[0])
    for c in u_in:
        c.wait_recv()
    u_in = hop(3)
    for i in FAR[5:]:
        send_tokens(0, i)
    for i in FAR:
        prepare(1, i)

    pltpu.make_async_copy(wrecv, wrecv, one_r.at[1]).wait()

    def add_rows(k, acc):
        return acc + wrecv[k].astype(f32)

    total_rows = lax.fori_loop(0, n_rep - 1, add_rows, wsel[r].astype(f32))
    local[4].wait()
    local[5].wait()
    share_g, share_u = gp_ref[0, 0], mom_ref[0, 0]
    for j in range(1, 4):
        share_g = jnp.where(frag == j, gp_ref[j, 0], share_g)
        share_u = jnp.where(frag == j, mom_ref[j, 0], share_u)
    delta = share_g - total_rows / n_rep
    u_new = outer_mom * share_u + delta
    g_new = share_g - outer_rate * (outer_mom * u_new + delta)
    gnew[...] = g_new

    def send_new(k, c):
        remote(gnew, grow.at[k - 1], one_s.at[2], one_r.at[2], {"rep": (r + k) % n_rep, "fsdp": f}).start()
        return c

    for c in u_in:
        c.wait_recv()
    u_in = hop(4)
    for i in FAR:
        send_tokens(1, i)
    lax.fori_loop(1, n_rep, send_new, 0)
    for j in range(4):
        ng_ref[j, 0] = jnp.where(frag == j, g_new, gp_ref[j, 0])
        nm_ref[j, 0] = jnp.where(frag == j, u_new, mom_ref[j, 0])

    def grad(t, first, count, cols):
        k = count * rows
        return lax.dot_general(
            t[first : first + count, :, cols].reshape(k, -1),
            u[first : first + count].reshape(k, feats),
            (((0,), (0,)), ((), ())),
            preferred_element_type=f32,
        )

    for i in FAR:
        t_in[0, i].wait_recv()
    for c in u_in:
        c.wait_recv()
    halves = (slice(0, 256), slice(256, 512))
    for m in halves:
        gsend[m, :] = grad(tp, 0, nz, m).astype(bf16)
    g_copy = keep(remote(gsend, grecv, one_s.at[3], one_r.at[3], partner))

    w_copy.wait_recv()

    def partial(i):
        return jnp.dot(tp[i], wp[...], preferred_element_type=f32) + jnp.dot(to[i], w[...], preferred_element_type=f32)

    vown[...] = partial(0)

    t_in[1, 7].wait_recv()
    vsend[0] = partial(7).astype(bf16)
    first_half, last_half = slice(0, rows // 2), slice(rows // 2, rows)
    v_in = [
        keep(remote(vsend.at[0, p], vrecv.at[0, p], v_s.at[n], v_r.at[n], zdev((1, nz - 1)[n])))
        for n, p in enumerate((first_half, last_half))
    ]
    for m in halves:
        gown[m, :] = grad(to, 0, 1, m) + grad(to, 7, 1, m)

    pltpu.make_async_copy(grow, grow, one_r.at[2]).wait()
    gfull[r] = gnew[...]

    def place(k, c):
        gfull[(r + n_rep - k) % n_rep] = grow[k - 1]
        return c

    lax.fori_loop(1, n_rep, place, 0)

    def ring(at, ahead, back):
        out = []
        for n, part in enumerate((ahead, back)):
            v_in[n].wait_recv()
            if at == 2:
                mine, other = (first_half, last_half)[n], (last_half, first_half)[n]
                vsend[at + n, mine] = (part[mine] + vrecv[0, mine].astype(f32)).astype(bf16)
                vsend[at + n, other] = part[other].astype(bf16)
            else:
                vsend[at + n] = (part + vrecv[at - 2 + n].astype(f32)).astype(bf16)
            out.append(
                keep(remote(vsend.at[at + n], vrecv.at[at + n], v_s.at[at + n], v_r.at[at + n], zdev((1, nz - 1)[n])))
            )
        return out

    t_in[1, 6].wait_recv()
    t_in[1, 5].wait_recv()
    v_in = ring(2, partial(6), partial(5))
    for m in halves:
        gown[m, :] += grad(to, 5, 2, m)

    t_in[1, 4].wait_recv()
    t_in[1, 3].wait_recv()
    v_in = ring(4, partial(4), partial(3))
    for m in halves:
        gown[m, :] += grad(to, 3, 2, m)

    g_copy.wait_recv()
    t_in[1, 1].wait_recv()
    t_in[1, 2].wait_recv()
    acc = jnp.zeros((8, feats), f32)
    for m in halves:
        g = gown[m, :] + grecv[m, :].astype(f32) + grad(to, 1, 2, m)
        gown[m, :] = g
        acc = acc + jnp.sum((g * g).reshape(32, 8, feats), axis=0)
    nsend[...] = acc[:, 0:128] + acc[:, 128:256] + acc[:, 256:384] + acc[:, 384:512]

    def send_norm(k, c):
        remote(nsend, nrecv.at[k - 1], one_s.at[4], one_r.at[4], {"rep": r, "fsdp": (f + k) % n_f}).start()
        return c

    lax.fori_loop(1, n_f, send_norm, 0)

    ahead_copy, back_copy = ring(6, partial(2), partial(1))

    local[6].wait()
    local[7].wait()
    pltpu.make_async_copy(nrecv, nrecv, one_r.at[4]).wait()
    tile = nsend[...] + jnp.sum(nrecv[...], axis=0)
    total = jnp.sum(jnp.sum(tile, axis=1, keepdims=True), axis=0, keepdims=True)
    factor = jnp.minimum(1.0, clip_bound / (jnp.sqrt(total) + 1e-06))

    def update(i, c):
        at = pl.ds(pl.multiple_of(i * 64, 64), 64)
        rows_new = gfull[pl.ds(i * 4, 4)].reshape(64, 128)
        for j in range(4):
            cols = slice(j * 128, (j + 1) * 128)
            clipped = gown[at, cols] * factor
            moment = 0.9 * fm[at, cols].astype(f32) + 0.1 * clipped
            square = 0.95 * sm[at, cols].astype(f32) + 0.05 * clipped * clipped
            wf = w[at, cols].astype(f32)
            inner = wf - inner_rate * (moment / (jnp.sqrt(square) + 1e-08) + decay_rate * wf)
            merged = blend * inner + (1.0 - blend) * rows_new
            nw[at, cols] = jnp.where(frag == j, merged, inner).astype(bf16)
        return c

    lax.fori_loop(0, 8, update, 0)

    ahead_copy.wait_recv()
    back_copy.wait_recv()
    val[...] = (vown[...] + vrecv[6].astype(f32) + vrecv[7].astype(f32)).astype(bf16)

    for c in copies:
        c.wait_send()
    pltpu.make_async_copy(wrecv, wrecv, one_s.at[1]).wait()
    pltpu.make_async_copy(grow, grow, one_s.at[2]).wait()
    pltpu.make_async_copy(nrecv, nrecv, one_s.at[4]).wait()


def hand_over(*refs):
    n = len(refs) // 2
    sems = refs[-1]
    copies = [pltpu.make_async_copy(refs[i], refs[n + i], sems.at[i]) for i in range(n)]
    for c in copies:
        c.start()
    for c in copies:
        c.wait()


def per_device(n_rep, n_fsdp, tokens, norm_gain, weights, first_moment, second_moment, upstream, global_params, outer_momentum, fragment):
    nz = n_fsdp // 2
    bf, f32 = jnp.bfloat16, jnp.float32
    vm, anywhere = pl.BlockSpec(memory_space=pltpu.VMEM), pl.BlockSpec(memory_space=pl.ANY)
    dma = pltpu.SemaphoreType.DMA
    out = pl.pallas_call(
        functools.partial(kernel, n_rep, nz),
        out_shape=(
            pltpu.VMEM((512, 512), bf),
            pltpu.VMEM((128, 512), bf),
            pltpu.VMEM(global_params.shape, f32),
            pltpu.VMEM(outer_momentum.shape, f32),
        ),
        in_specs=[anywhere] * 8 + [pl.BlockSpec(memory_space=pltpu.SMEM)],
        out_specs=(vm,) * 4,
        scratch_shapes=[
            pltpu.VMEM((128, 8192), bf),
            pltpu.VMEM((14, 128, 512), bf),
            pltpu.VMEM((8, 128, 512), bf),
            pltpu.VMEM((8, 128, 512), bf),
            pltpu.VMEM((512, 512), bf),
            pltpu.VMEM((512, 512), bf),
            pltpu.VMEM((8, 128, 512), bf),
            pltpu.VMEM((512, 512), bf),
            pltpu.VMEM((512, 512), bf),
            pltpu.VMEM((64, 128), f32),
            pltpu.VMEM(global_params.shape, f32),
            pltpu.VMEM(outer_momentum.shape, f32),
            pltpu.VMEM((512, 512), f32),
            pltpu.VMEM((512, 512), bf),
            pltpu.VMEM((512, 512), bf),
            pltpu.VMEM((8, 128, 512), bf),
            pltpu.VMEM((8, 128, 512), bf),
            pltpu.VMEM((128, 512), f32),
            pltpu.VMEM((128, 128), f32),
            pltpu.VMEM((n_rep, 16, 128), bf),
            pltpu.VMEM((n_rep - 1, 16, 128), bf),
            pltpu.VMEM((16, 128), f32),
            pltpu.VMEM((n_rep - 1, 16, 128), f32),
            pltpu.VMEM((n_rep, 16, 128), f32),
            pltpu.VMEM((8, 128), f32),
            pltpu.VMEM((n_fsdp - 1, 8, 128), f32),
            dma((8,)),
            dma((14,)),
            dma((14,)),
            dma((8,)),
            dma((8,)),
            dma((8,)),
            dma((8,)),
            dma((5,)),
            dma((5,)),
        ],
        compiler_params=pltpu.CompilerParams(collective_id=0, has_side_effects=True, vmem_limit_bytes=40 * 1024 * 1024),
        name="step",
    )(
        *(
            pltpu.with_memory_space_constraint(a, pltpu.HBM)
            for a in (
                tokens[0],
                norm_gain.reshape(64, 128),
                weights[0],
                first_moment[0],
                second_moment[0],
                upstream[0],
                global_params,
                outer_momentum,
            )
        ),
        fragment,
    )
    out = pl.pallas_call(
        hand_over,
        out_shape=tuple(pltpu.HBM(o.shape, o.dtype) for o in out),
        in_specs=[vm] * 4,
        out_specs=(anywhere,) * 4,
        scratch_shapes=[dma((4,))],
        name="hand_over",
    )(*(pltpu.with_memory_space_constraint(o, pltpu.VMEM) for o in out))
    return (out[0][None], out[1][None], out[2], out[3])


def solution(mesh):
    placed = (
        P("rep", "fsdp", None),
        P(),
        P("rep", "fsdp", None),
        P("rep", "fsdp", None),
        P("rep", "fsdp", None),
        P("rep", "fsdp", None),
        P(None, "fsdp", "rep", None),
        P(None, "fsdp", "rep", None),
        P(),
    )
    return jax.shard_map(
        functools.partial(per_device, mesh.shape["rep"], mesh.shape["fsdp"]),
        mesh=mesh,
        in_specs=placed,
        out_specs=(
            P("rep", "fsdp", None),
            P("rep", "fsdp", None),
            P(None, "fsdp", "rep", None),
            P(None, "fsdp", "rep", None),
        ),
        check_vma=False,
    )
```

```python
import functools

import jax
import jax.numpy as jnp
from jax import lax
from jax.experimental import pallas as pl
from jax.experimental.pallas import tpu as pltpu
from jax.sharding import PartitionSpec as P

MESH = pl.DeviceIdType.MESH

clip_bound = 1.0
inner_rate = 0.02
decay_rate = 0.1
outer_rate = 0.7
outer_mom = 0.9
blend = 0.5

ORDER = (1, 7, 2, 6, 3, 5, 4)
AHEAD, BACK = (0, 1, 3, 5, 7), (0, 2, 4, 6, 7)


def kernel(
    n_rep,
    nz,
    tok_hbm,
    gain_hbm,
    w_hbm,
    fm_hbm,
    sm_hbm,
    u_hbm,
    gp_hbm,
    mom_hbm,
    frag_ref,
    nw,
    val,
    ng_ref,
    nm_ref,
    x,
    xn,
    tp,
    to,
    w,
    wp,
    u,
    fm,
    sm,
    gain_ref,
    gp_ref,
    mom_ref,
    gown,
    gsend,
    grecv,
    vsend,
    vrecv,
    vown,
    scale_ref,
    wsel,
    wrecv,
    gnew,
    grow,
    gfull,
    nsend,
    nrecv,
    loc,
    t_s,
    t_r,
    u_s,
    u_r,
    v_s,
    v_r,
    one_s,
    one_r,
    hello,
):
    r = lax.axis_index("rep")
    f = lax.axis_index("fsdp")
    y, z = f // nz, f % nz
    n_f = 2 * nz
    rows, feats = 128, 512
    f32, bf16 = jnp.float32, jnp.bfloat16

    def zdev(k):
        return {"rep": r, "fsdp": y * nz + (z + k) % nz}

    partner = {"rep": r, "fsdp": (1 - y) * nz + z}

    def remote(src, dst, send_sem, recv_sem, device):
        return pltpu.make_async_remote_copy(
            src_ref=src, dst_ref=dst, send_sem=send_sem, recv_sem=recv_sem, device_id=device, device_id_type=MESH
        )

    barrier = pltpu.get_barrier_semaphore()

    def greet_f(k, c):
        pl.semaphore_signal(barrier, inc=1, device_id={"rep": r, "fsdp": (f + k) % n_f}, device_id_type=MESH)
        return c

    half = n_rep // 2
    rank = (r % 2) * half + r // 2

    def at_rank(q):
        return {"rep": (q % half) * 2 + q // half, "fsdp": f}

    def greet_r(q, c):
        pl.semaphore_signal(barrier, inc=1, device_id=at_rank(q), device_id_type=MESH)
        return c

    def say_hello(q, c):
        pl.semaphore_signal(hello, inc=1, device_id=at_rank(q), device_id_type=MESH)
        return c

    local = [
        pltpu.make_async_copy(src, dst, loc.at[n])
        for n, (src, dst) in enumerate(
            (
                (u_hbm, u.at[0]),
                (w_hbm, w),
                (tok_hbm, x),
                (gain_hbm, gain_ref),
                (gp_hbm, gp_ref),
                (mom_hbm, mom_ref),
                (fm_hbm, fm),
                (sm_hbm, sm),
            )
        )
    ]
    for c in local:
        c.start()
    lax.fori_loop(1, n_f, greet_f, 0)
    lax.fori_loop(rank + 1, n_rep, greet_r, 0)

    copies = []

    def keep(c):
        c.start()
        copies.append(c)
        return c

    def hop(h):
        part = [slice(0, rows), slice(0, rows)] if h < 4 else [slice(0, rows // 2), slice(rows // 2, rows)]
        return [
            keep(remote(u.at[s[h - 1], p], u.at[s[h], p], u_s.at[2 * h - 2 + n], u_r.at[2 * h - 2 + n], zdev((1, nz - 1)[n])))
            for n, (s, p) in enumerate(zip((AHEAD, BACK), part))
        ]

    local[0].wait()
    pl.semaphore_wait(barrier, n_f - 1 + rank)
    u_in = hop(1)
    local[1].wait()
    w_copy = keep(remote(w, wp, one_s.at[0], one_r.at[0], partner))
    local[2].wait()

    def squares(i, acc):
        for j in range(4):
            v = x[:, pl.ds(pl.multiple_of(i * 512 + j * 128, 128), 128)].astype(f32)
            acc = acc + v * v
        return acc

    acc = lax.fori_loop(0, 2 * nz, squares, jnp.zeros((rows, 128), f32))
    mean = jnp.sum(acc, axis=1, keepdims=True) / (2 * nz * feats)
    scale_ref[...] = jnp.broadcast_to(lax.rsqrt(mean + 1e-05), (rows, 128))

    def normed(block, dst):
        for j in range(4):
            g = gain_ref[pl.ds(block * 4 + j, 1), :]
            v = x[:, pl.ds(pl.multiple_of(block * feats + j * 128, 128), 128)].astype(f32)
            dst[:, j * 128 : (j + 1) * 128] = (v * scale_ref[...] * g).astype(bf16)

    t_in = {}

    def prepare(kind, i):
        block = (1 - y if kind == 0 else y) * nz + (z + ORDER[i - 1]) % nz
        normed(block, xn.at[kind * 7 + i - 1])

    def send_tokens(kind, i):
        n = kind * 7 + i - 1
        t_in[kind, i] = keep(remote(xn.at[n], (to if kind else tp).at[i], t_s.at[n], t_r.at[n], zdev(ORDER[i - 1])))

    def send_rows(k, c):
        dst = (r + k) % n_rep
        remote(wsel.at[dst], wrecv.at[k - 1], one_s.at[1], one_r.at[1], {"rep": dst, "fsdp": f}).start()
        return c

    def wait_all(cs):
        for c in cs:
            c.wait_recv()

    def grad(t, first, count, cols):
        k = count * rows
        return lax.dot_general(
            t[first : first + count, :, cols].reshape(k, -1),
            u[first : first + count].reshape(k, feats),
            (((0,), (0,)), ((), ())),
            preferred_element_type=f32,
        )

    def partial(i):
        return jnp.dot(tp[i], wp[...], preferred_element_type=f32) + jnp.dot(to[i], w[...], preferred_element_type=f32)

    def wait_tokens(*slots):
        for i in slots:
            t_in[0, i].wait_recv()
            t_in[1, i].wait_recv()

    halves = (slice(0, 256), slice(256, 512))
    first_half, last_half = slice(0, rows // 2), slice(rows // 2, rows)

    def ring(at, ahead, back):
        out = []
        for n, part in enumerate((ahead, back)):
            v_in[n].wait_recv()
            if at == 2:
                mine, other = (first_half, last_half)[n], (last_half, first_half)[n]
                vsend[at + n, mine] = (part[mine] + vrecv[0, mine].astype(f32)).astype(bf16)
                vsend[at + n, other] = part[other].astype(bf16)
            else:
                vsend[at + n] = (part + vrecv[at - 2 + n].astype(f32)).astype(bf16)
            out.append(
                keep(remote(vsend.at[at + n], vrecv.at[at + n], v_s.at[at + n], v_r.at[at + n], zdev((1, nz - 1)[n])))
            )
        return out

    local[3].wait()
    for i in (7, 5, 6):
        prepare(0, i)
        send_tokens(0, i)
    frag = frag_ref[0]
    sel = w[:, 0:128]
    for j in range(1, 4):
        sel = jnp.where(frag == j, w[:, j * 128 : (j + 1) * 128], sel)
    wsel[...] = sel.reshape(wsel.shape)
    lax.fori_loop(0, rank, say_hello, 0)
    for i in (3, 4, 1, 2):
        prepare(0, i)

    wait_all(u_in)
    u_in = hop(2)
    send_tokens(0, 3)
    send_tokens(0, 4)
    normed((1 - y) * nz + z, tp.at[0])
    normed(y * nz + z, to.at[0])
    for i in (7, 5, 6):
        prepare(1, i)
    wait_all(u_in)
    u_in = hop(3)
    send_tokens(0, 1)
    send_tokens(0, 2)

    @pl.when(rank < n_rep - 1)
    def _():
        pl.semaphore_wait(hello, n_rep - 1 - rank)

    lax.fori_loop(1, n_rep, send_rows, 0)
    for i in (3, 4, 1, 2):
        prepare(1, i)
    w_copy.wait_recv()
    vown[...] = partial(0)
    wait_all(u_in)
    u_in = hop(4)
    send_tokens(1, 7)
    send_tokens(1, 5)
    send_tokens(1, 6)
    for i in (7, 5, 6, 3, 4, 1, 2):
        t_in[0, i].wait_recv()
    wait_all(u_in)
    for m in halves:
        gsend[m, :] = grad(tp, 0, nz, m).astype(bf16)
    g_copy = keep(remote(gsend, grecv, one_s.at[3], one_r.at[3], partner))
    t_in[1, 7].wait_recv()
    vsend[0] = partial(7).astype(bf16)
    v_in = [
        keep(remote(vsend.at[0, p], vrecv.at[0, p], v_s.at[n], v_r.at[n], zdev((1, nz - 1)[n])))
        for n, p in enumerate((first_half, last_half))
    ]
    send_tokens(1, 3)
    send_tokens(1, 4)
    for m in halves:
        gown[m, :] = grad(to, 0, 1, m) + grad(to, 7, 1, m)
    pltpu.make_async_copy(wrecv, wrecv, one_r.at[1]).wait()

    def add_rows(k, acc):
        return acc + wrecv[k].astype(f32)

    total_rows = lax.fori_loop(0, n_rep - 1, add_rows, wsel[r].astype(f32))
    local[4].wait()
    local[5].wait()
    share_g, share_u = gp_ref[0, 0], mom_ref[0, 0]
    for j in range(1, 4):
        share_g = jnp.where(frag == j, gp_ref[j, 0], share_g)
        share_u = jnp.where(frag == j, mom_ref[j, 0], share_u)
    delta = share_g - total_rows / n_rep
    u_new = outer_mom * share_u + delta
    g_new = share_g - outer_rate * (outer_mom * u_new + delta)
    gnew[...] = g_new

    def send_new(k, c):
        remote(gnew, grow.at[k - 1], one_s.at[2], one_r.at[2], {"rep": (r + k) % n_rep, "fsdp": f}).start()
        return c

    lax.fori_loop(1, n_rep, send_new, 0)
    for j in range(4):
        ng_ref[j, 0] = jnp.where(frag == j, g_new, gp_ref[j, 0])
        nm_ref[j, 0] = jnp.where(frag == j, u_new, mom_ref[j, 0])

    t_in[1, 6].wait_recv()
    t_in[1, 5].wait_recv()
    v_in = ring(2, partial(6), partial(5))
    send_tokens(1, 1)
    send_tokens(1, 2)
    for m in halves:
        gown[m, :] += grad(to, 5, 2, m)
    t_in[1, 4].wait_recv()
    t_in[1, 3].wait_recv()
    v_in = ring(4, partial(4), partial(3))
    for m in halves:
        gown[m, :] += grad(to, 3, 2, m)
    t_in[1, 1].wait_recv()
    t_in[1, 2].wait_recv()
    g_copy.wait_recv()
    acc = jnp.zeros((8, feats), f32)
    for m in halves:
        g = gown[m, :] + grecv[m, :].astype(f32) + grad(to, 1, 2, m)
        gown[m, :] = g
        acc = acc + jnp.sum((g * g).reshape(32, 8, feats), axis=0)
    nsend[...] = acc[:, 0:128] + acc[:, 128:256] + acc[:, 256:384] + acc[:, 384:512]

    def send_norm(k, c):
        remote(nsend, nrecv.at[k - 1], one_s.at[4], one_r.at[4], {"rep": r, "fsdp": (f + k) % n_f}).start()
        return c

    lax.fori_loop(1, n_f, send_norm, 0)

    v_in = ring(6, partial(2), partial(1))
    pltpu.make_async_copy(grow, grow, one_r.at[2]).wait()
    gfull[r] = gnew[...]

    def place(k, c):
        gfull[(r + n_rep - k) % n_rep] = grow[k - 1]
        return c

    lax.fori_loop(1, n_rep, place, 0)

    local[6].wait()
    local[7].wait()
    pltpu.make_async_copy(nrecv, nrecv, one_r.at[4]).wait()
    tile = nsend[...] + jnp.sum(nrecv[...], axis=0)
    total = jnp.sum(jnp.sum(tile, axis=1, keepdims=True), axis=0, keepdims=True)
    factor = jnp.minimum(1.0, clip_bound / (jnp.sqrt(total) + 1e-06))

    def update(i, c):
        at = pl.ds(pl.multiple_of(i * 64, 64), 64)
        rows_new = gfull[pl.ds(i * 4, 4)].reshape(64, 128)
        for j in range(4):
            cols = slice(j * 128, (j + 1) * 128)
            clipped = gown[at, cols] * factor
            moment = 0.9 * fm[at, cols].astype(f32) + 0.1 * clipped
            square = 0.95 * sm[at, cols].astype(f32) + 0.05 * clipped * clipped
            wf = w[at, cols].astype(f32)
            inner = wf - inner_rate * (moment / (jnp.sqrt(square) + 1e-08) + decay_rate * wf)
            merged = blend * inner + (1.0 - blend) * rows_new
            nw[at, cols] = jnp.where(frag == j, merged, inner).astype(bf16)
        return c

    lax.fori_loop(0, 8, update, 0)

    wait_all(v_in)
    val[...] = (vown[...] + vrecv[6].astype(f32) + vrecv[7].astype(f32)).astype(bf16)

    for c in copies:
        c.wait_send()
    pltpu.make_async_copy(wrecv, wrecv, one_s.at[1]).wait()
    pltpu.make_async_copy(grow, grow, one_s.at[2]).wait()
    pltpu.make_async_copy(nrecv, nrecv, one_s.at[4]).wait()


def hand_over(*refs):
    n = len(refs) // 2
    sems = refs[-1]
    copies = [pltpu.make_async_copy(refs[i], refs[n + i], sems.at[i]) for i in range(n)]
    for c in copies:
        c.start()
    for c in copies:
        c.wait()


def per_device(n_rep, n_fsdp, tokens, norm_gain, weights, first_moment, second_moment, upstream, global_params, outer_momentum, fragment):
    nz = n_fsdp // 2
    bf, f32 = jnp.bfloat16, jnp.float32
    vm, anywhere = pl.BlockSpec(memory_space=pltpu.VMEM), pl.BlockSpec(memory_space=pl.ANY)
    dma = pltpu.SemaphoreType.DMA
    out = pl.pallas_call(
        functools.partial(kernel, n_rep, nz),
        out_shape=(
            pltpu.VMEM((512, 512), bf),
            pltpu.VMEM((128, 512), bf),
            pltpu.VMEM(global_params.shape, f32),
            pltpu.VMEM(outer_momentum.shape, f32),
        ),
        in_specs=[anywhere] * 8 + [pl.BlockSpec(memory_space=pltpu.SMEM)],
        out_specs=(vm,) * 4,
        scratch_shapes=[
            pltpu.VMEM((128, 8192), bf),
            pltpu.VMEM((14, 128, 512), bf),
            pltpu.VMEM((8, 128, 512), bf),
            pltpu.VMEM((8, 128, 512), bf),
            pltpu.VMEM((512, 512), bf),
            pltpu.VMEM((512, 512), bf),
            pltpu.VMEM((8, 128, 512), bf),
            pltpu.VMEM((512, 512), bf),
            pltpu.VMEM((512, 512), bf),
            pltpu.VMEM((64, 128), f32),
            pltpu.VMEM(global_params.shape, f32),
            pltpu.VMEM(outer_momentum.shape, f32),
            pltpu.VMEM((512, 512), f32),
            pltpu.VMEM((512, 512), bf),
            pltpu.VMEM((512, 512), bf),
            pltpu.VMEM((8, 128, 512), bf),
            pltpu.VMEM((8, 128, 512), bf),
            pltpu.VMEM((128, 512), f32),
            pltpu.VMEM((128, 128), f32),
            pltpu.VMEM((n_rep, 16, 128), bf),
            pltpu.VMEM((n_rep - 1, 16, 128), bf),
            pltpu.VMEM((16, 128), f32),
            pltpu.VMEM((n_rep - 1, 16, 128), f32),
            pltpu.VMEM((n_rep, 16, 128), f32),
            pltpu.VMEM((8, 128), f32),
            pltpu.VMEM((n_fsdp - 1, 8, 128), f32),
            dma((8,)),
            dma((14,)),
            dma((14,)),
            dma((8,)),
            dma((8,)),
            dma((8,)),
            dma((8,)),
            dma((5,)),
            dma((5,)),
            pltpu.SemaphoreType.REGULAR,
        ],
        compiler_params=pltpu.CompilerParams(collective_id=0, has_side_effects=True, vmem_limit_bytes=40 * 1024 * 1024),
        name="step",
    )(
        *(
            pltpu.with_memory_space_constraint(a, pltpu.HBM)
            for a in (
                tokens[0],
                norm_gain.reshape(64, 128),
                weights[0],
                first_moment[0],
                second_moment[0],
                upstream[0],
                global_params,
                outer_momentum,
            )
        ),
        fragment,
    )
    out = pl.pallas_call(
        hand_over,
        out_shape=tuple(pltpu.HBM(o.shape, o.dtype) for o in out),
        in_specs=[vm] * 4,
        out_specs=(anywhere,) * 4,
        scratch_shapes=[dma((4,))],
        name="hand_over",
    )(*(pltpu.with_memory_space_constraint(o, pltpu.VMEM) for o in out))
    return (out[0][None], out[1][None], out[2], out[3])


def solution(mesh):
    placed = (
        P("rep", "fsdp", None),
        P(),
        P("rep", "fsdp", None),
        P("rep", "fsdp", None),
        P("rep", "fsdp", None),
        P("rep", "fsdp", None),
        P(None, "fsdp", "rep", None),
        P(None, "fsdp", "rep", None),
        P(),
    )
    return jax.shard_map(
        functools.partial(per_device, mesh.shape["rep"], mesh.shape["fsdp"]),
        mesh=mesh,
        in_specs=placed,
        out_specs=(
            P("rep", "fsdp", None),
            P("rep", "fsdp", None),
            P(None, "fsdp", "rep", None),
            P(None, "fsdp", "rep", None),
        ),
        check_vma=False,
    )
```

```python
import functools

import jax
import jax.numpy as jnp
from jax import lax
from jax.experimental import pallas as pl
from jax.experimental.pallas import tpu as pltpu
from jax.sharding import PartitionSpec as P

MESH = pl.DeviceIdType.MESH

clip_bound = 1.0
inner_rate = 0.02
decay_rate = 0.1
outer_rate = 0.7
outer_mom = 0.9
blend = 0.5

ORDER = (1, 7, 2, 6, 3, 5, 4)
AHEAD, BACK = (0, 1, 3, 5, 7), (0, 2, 4, 6, 7)


def kernel(
    n_rep,
    nz,
    tok_hbm,
    gain_hbm,
    w_hbm,
    fm_hbm,
    sm_hbm,
    u_hbm,
    gp_hbm,
    mom_hbm,
    frag_ref,
    nw,
    val,
    ng_ref,
    nm_ref,
    x,
    xn,
    tp,
    to,
    w,
    wp,
    u,
    fm,
    sm,
    gain_ref,
    gp_ref,
    mom_ref,
    gown,
    gsend,
    grecv,
    vsend,
    vrecv,
    vown,
    scale_ref,
    wsel,
    wrecv,
    gnew,
    grow,
    gfull,
    nsend,
    nrecv,
    loc,
    t_s,
    t_r,
    u_s,
    u_r,
    v_s,
    v_r,
    one_s,
    one_r,
    hello,
):
    r = lax.axis_index("rep")
    f = lax.axis_index("fsdp")
    y, z = f // nz, f % nz
    n_f = 2 * nz
    rows, feats = 128, 512
    f32, bf16 = jnp.float32, jnp.bfloat16

    def zdev(k):
        return {"rep": r, "fsdp": y * nz + (z + k) % nz}

    partner = {"rep": r, "fsdp": (1 - y) * nz + z}

    def remote(src, dst, send_sem, recv_sem, device):
        return pltpu.make_async_remote_copy(
            src_ref=src, dst_ref=dst, send_sem=send_sem, recv_sem=recv_sem, device_id=device, device_id_type=MESH
        )

    barrier = pltpu.get_barrier_semaphore()

    def greet_f(k, c):
        pl.semaphore_signal(barrier, inc=1, device_id={"rep": r, "fsdp": (f + k) % n_f}, device_id_type=MESH)
        return c

    half, quad = n_rep // 2, n_rep // 8
    rank = (r % 2) * half + (r // 2 % 4) * quad + r // 8

    def at_rank(q):
        return {"rep": (q % quad) * 8 + (q % half) // quad * 2 + q // half, "fsdp": f}

    def greet_r(q, c):
        pl.semaphore_signal(barrier, inc=1, device_id=at_rank(q), device_id_type=MESH)
        return c

    def say_hello(q, c):
        pl.semaphore_signal(hello, inc=1, device_id=at_rank(q), device_id_type=MESH)
        return c

    local = [
        pltpu.make_async_copy(src, dst, loc.at[n])
        for n, (src, dst) in enumerate(
            (
                (u_hbm, u.at[0]),
                (w_hbm, w),
                (tok_hbm, x),
                (gain_hbm, gain_ref),
                (gp_hbm, gp_ref),
                (mom_hbm, mom_ref),
                (fm_hbm, fm),
                (sm_hbm, sm),
            )
        )
    ]
    for c in local:
        c.start()
    lax.fori_loop(1, n_f, greet_f, 0)
    lax.fori_loop(rank + 1, n_rep, greet_r, 0)

    copies = []

    def keep(c):
        c.start()
        copies.append(c)
        return c

    def hop(h):
        part = [slice(0, rows), slice(0, rows)] if h < 4 else [slice(0, rows // 2), slice(rows // 2, rows)]
        return [
            keep(remote(u.at[s[h - 1], p], u.at[s[h], p], u_s.at[2 * h - 2 + n], u_r.at[2 * h - 2 + n], zdev((1, nz - 1)[n])))
            for n, (s, p) in enumerate(zip((AHEAD, BACK), part))
        ]

    local[0].wait()
    pl.semaphore_wait(barrier, n_f - 1 + rank)
    u_in = hop(1)
    local[1].wait()
    w_copy = keep(remote(w, wp, one_s.at[0], one_r.at[0], partner))
    local[2].wait()

    def squares(i, acc):
        for j in range(4):
            v = x[:, pl.ds(pl.multiple_of(i * 512 + j * 128, 128), 128)].astype(f32)
            acc = acc + v * v
        return acc

    acc = lax.fori_loop(0, 2 * nz, squares, jnp.zeros((rows, 128), f32))
    mean = jnp.sum(acc, axis=1, keepdims=True) / (2 * nz * feats)
    scale_ref[...] = jnp.broadcast_to(lax.rsqrt(mean + 1e-05), (rows, 128))

    def normed(block, dst):
        for j in range(4):
            g = gain_ref[pl.ds(block * 4 + j, 1), :]
            v = x[:, pl.ds(pl.multiple_of(block * feats + j * 128, 128), 128)].astype(f32)
            dst[:, j * 128 : (j + 1) * 128] = (v * scale_ref[...] * g).astype(bf16)

    t_in = {}

    def prepare(kind, i):
        block = (1 - y if kind == 0 else y) * nz + (z + ORDER[i - 1]) % nz
        normed(block, xn.at[kind * 7 + i - 1])

    def send_tokens(kind, i):
        n = kind * 7 + i - 1
        t_in[kind, i] = keep(remote(xn.at[n], (to if kind else tp).at[i], t_s.at[n], t_r.at[n], zdev(ORDER[i - 1])))

    def send_rows(k, c):
        dst = (r + k) % n_rep
        remote(wsel.at[dst], wrecv.at[k - 1], one_s.at[1], one_r.at[1], {"rep": dst, "fsdp": f}).start()
        return c

    def wait_all(cs):
        for c in cs:
            c.wait_recv()

    def grad(t, first, count, cols):
        k = count * rows
        return lax.dot_general(
            t[first : first + count, :, cols].reshape(k, -1),
            u[first : first + count].reshape(k, feats),
            (((0,), (0,)), ((), ())),
            preferred_element_type=f32,
        )

    def partial(i):
        return jnp.dot(tp[i], wp[...], preferred_element_type=f32) + jnp.dot(to[i], w[...], preferred_element_type=f32)

    def wait_tokens(*slots):
        for i in slots:
            t_in[0, i].wait_recv()
            t_in[1, i].wait_recv()

    halves = (slice(0, 256), slice(256, 512))
    first_half, last_half = slice(0, rows // 2), slice(rows // 2, rows)

    def ring(at, ahead, back):
        out = []
        for n, part in enumerate((ahead, back)):
            v_in[n].wait_recv()
            if at == 2:
                mine, other = (first_half, last_half)[n], (last_half, first_half)[n]
                vsend[at + n, mine] = (part[mine] + vrecv[0, mine].astype(f32)).astype(bf16)
                vsend[at + n, other] = part[other].astype(bf16)
            else:
                vsend[at + n] = (part + vrecv[at - 2 + n].astype(f32)).astype(bf16)
            out.append(
                keep(remote(vsend.at[at + n], vrecv.at[at + n], v_s.at[at + n], v_r.at[at + n], zdev((1, nz - 1)[n])))
            )
        return out

    local[3].wait()
    for i in (7, 5, 6):
        prepare(0, i)
        send_tokens(0, i)
    frag = frag_ref[0]
    sel = w[:, 0:128]
    for j in range(1, 4):
        sel = jnp.where(frag == j, w[:, j * 128 : (j + 1) * 128], sel)
    wsel[...] = sel.reshape(wsel.shape)
    lax.fori_loop(0, rank, say_hello, 0)
    for i in (3, 4, 1, 2):
        prepare(0, i)

    wait_all(u_in)
    u_in = hop(2)
    send_tokens(0, 3)
    send_tokens(0, 4)
    normed((1 - y) * nz + z, tp.at[0])
    normed(y * nz + z, to.at[0])
    for i in (7, 5, 6):
        prepare(1, i)
    wait_all(u_in)
    u_in = hop(3)
    send_tokens(0, 1)
    send_tokens(0, 2)

    @pl.when(rank < n_rep - 1)
    def _():
        pl.semaphore_wait(hello, n_rep - 1 - rank)

    lax.fori_loop(1, n_rep, send_rows, 0)
    for i in (3, 4, 1, 2):
        prepare(1, i)
    w_copy.wait_recv()
    vown[...] = partial(0)
    wait_all(u_in)
    u_in = hop(4)
    send_tokens(1, 7)
    for i in (7, 5, 6):
        t_in[0, i].wait_recv()
    send_tokens(1, 5)
    send_tokens(1, 6)
    for i in (3, 4, 1, 2):
        t_in[0, i].wait_recv()
    wait_all(u_in)
    for m in halves:
        gsend[m, :] = grad(tp, 0, nz, m).astype(bf16)
    g_copy = keep(remote(gsend, grecv, one_s.at[3], one_r.at[3], partner))
    t_in[1, 7].wait_recv()
    vsend[0] = partial(7).astype(bf16)
    v_in = [
        keep(remote(vsend.at[0, p], vrecv.at[0, p], v_s.at[n], v_r.at[n], zdev((1, nz - 1)[n])))
        for n, p in enumerate((first_half, last_half))
    ]
    for m in halves:
        gown[m, :] = grad(to, 0, 1, m) + grad(to, 7, 1, m)
    send_tokens(1, 3)
    send_tokens(1, 4)
    t_in[1, 6].wait_recv()
    t_in[1, 5].wait_recv()
    v_in = ring(2, partial(6), partial(5))
    pltpu.make_async_copy(wrecv, wrecv, one_r.at[1]).wait()

    def add_rows(k, acc):
        return acc + wrecv[k].astype(f32)

    total_rows = lax.fori_loop(0, n_rep - 1, add_rows, wsel[r].astype(f32))
    local[4].wait()
    local[5].wait()
    share_g, share_u = gp_ref[0, 0], mom_ref[0, 0]
    for j in range(1, 4):
        share_g = jnp.where(frag == j, gp_ref[j, 0], share_g)
        share_u = jnp.where(frag == j, mom_ref[j, 0], share_u)
    delta = share_g - total_rows / n_rep
    u_new = outer_mom * share_u + delta
    g_new = share_g - outer_rate * (outer_mom * u_new + delta)
    gnew[...] = g_new

    def send_new(k, c):
        remote(gnew, grow.at[k - 1], one_s.at[2], one_r.at[2], {"rep": (r + k) % n_rep, "fsdp": f}).start()
        return c

    lax.fori_loop(1, n_rep, send_new, 0)
    for j in range(4):
        ng_ref[j, 0] = jnp.where(frag == j, g_new, gp_ref[j, 0])
        nm_ref[j, 0] = jnp.where(frag == j, u_new, mom_ref[j, 0])

    for m in halves:
        gown[m, :] += grad(to, 5, 2, m)
    t_in[1, 4].wait_recv()
    t_in[1, 3].wait_recv()
    send_tokens(1, 1)
    send_tokens(1, 2)
    v_in = ring(4, partial(4), partial(3))
    for m in halves:
        gown[m, :] += grad(to, 3, 2, m)
    t_in[1, 1].wait_recv()
    t_in[1, 2].wait_recv()
    g_copy.wait_recv()
    acc = jnp.zeros((8, feats), f32)
    for m in halves:
        g = gown[m, :] + grecv[m, :].astype(f32) + grad(to, 1, 2, m)
        gown[m, :] = g
        acc = acc + jnp.sum((g * g).reshape(32, 8, feats), axis=0)
    nsend[...] = acc[:, 0:128] + acc[:, 128:256] + acc[:, 256:384] + acc[:, 384:512]

    def send_norm(k, c):
        remote(nsend, nrecv.at[k - 1], one_s.at[4], one_r.at[4], {"rep": r, "fsdp": (f + k) % n_f}).start()
        return c

    lax.fori_loop(1, n_f, send_norm, 0)

    v_in = ring(6, partial(2), partial(1))
    pltpu.make_async_copy(grow, grow, one_r.at[2]).wait()
    gfull[r] = gnew[...]

    def place(k, c):
        gfull[(r + n_rep - k) % n_rep] = grow[k - 1]
        return c

    lax.fori_loop(1, n_rep, place, 0)

    local[6].wait()
    local[7].wait()
    pltpu.make_async_copy(nrecv, nrecv, one_r.at[4]).wait()
    tile = nsend[...] + jnp.sum(nrecv[...], axis=0)
    total = jnp.sum(jnp.sum(tile, axis=1, keepdims=True), axis=0, keepdims=True)
    factor = jnp.minimum(1.0, clip_bound / (jnp.sqrt(total) + 1e-06))

    def update(i, c):
        at = pl.ds(pl.multiple_of(i * 64, 64), 64)
        rows_new = gfull[pl.ds(i * 4, 4)].reshape(64, 128)
        for j in range(4):
            cols = slice(j * 128, (j + 1) * 128)
            clipped = gown[at, cols] * factor
            moment = 0.9 * fm[at, cols].astype(f32) + 0.1 * clipped
            square = 0.95 * sm[at, cols].astype(f32) + 0.05 * clipped * clipped
            wf = w[at, cols].astype(f32)
            inner = wf - inner_rate * (moment / (jnp.sqrt(square) + 1e-08) + decay_rate * wf)
            merged = blend * inner + (1.0 - blend) * rows_new
            nw[at, cols] = jnp.where(frag == j, merged, inner).astype(bf16)
        return c

    lax.fori_loop(0, 8, update, 0)

    wait_all(v_in)
    val[...] = (vown[...] + vrecv[6].astype(f32) + vrecv[7].astype(f32)).astype(bf16)

    for c in copies:
        c.wait_send()
    pltpu.make_async_copy(wrecv, wrecv, one_s.at[1]).wait()
    pltpu.make_async_copy(grow, grow, one_s.at[2]).wait()
    pltpu.make_async_copy(nrecv, nrecv, one_s.at[4]).wait()


def hand_over(*refs):
    n = len(refs) // 2
    sems = refs[-1]
    copies = [pltpu.make_async_copy(refs[i], refs[n + i], sems.at[i]) for i in range(n)]
    for c in copies:
        c.start()
    for c in copies:
        c.wait()


def per_device(n_rep, n_fsdp, tokens, norm_gain, weights, first_moment, second_moment, upstream, global_params, outer_momentum, fragment):
    nz = n_fsdp // 2
    bf, f32 = jnp.bfloat16, jnp.float32
    vm, anywhere = pl.BlockSpec(memory_space=pltpu.VMEM), pl.BlockSpec(memory_space=pl.ANY)
    dma = pltpu.SemaphoreType.DMA
    out = pl.pallas_call(
        functools.partial(kernel, n_rep, nz),
        out_shape=(
            pltpu.VMEM((512, 512), bf),
            pltpu.VMEM((128, 512), bf),
            pltpu.VMEM(global_params.shape, f32),
            pltpu.VMEM(outer_momentum.shape, f32),
        ),
        in_specs=[anywhere] * 8 + [pl.BlockSpec(memory_space=pltpu.SMEM)],
        out_specs=(vm,) * 4,
        scratch_shapes=[
            pltpu.VMEM((128, 8192), bf),
            pltpu.VMEM((14, 128, 512), bf),
            pltpu.VMEM((8, 128, 512), bf),
            pltpu.VMEM((8, 128, 512), bf),
            pltpu.VMEM((512, 512), bf),
            pltpu.VMEM((512, 512), bf),
            pltpu.VMEM((8, 128, 512), bf),
            pltpu.VMEM((512, 512), bf),
            pltpu.VMEM((512, 512), bf),
            pltpu.VMEM((64, 128), f32),
            pltpu.VMEM(global_params.shape, f32),
            pltpu.VMEM(outer_momentum.shape, f32),
            pltpu.VMEM((512, 512), f32),
            pltpu.VMEM((512, 512), bf),
            pltpu.VMEM((512, 512), bf),
            pltpu.VMEM((8, 128, 512), bf),
            pltpu.VMEM((8, 128, 512), bf),
            pltpu.VMEM((128, 512), f32),
            pltpu.VMEM((128, 128), f32),
            pltpu.VMEM((n_rep, 16, 128), bf),
            pltpu.VMEM((n_rep - 1, 16, 128), bf),
            pltpu.VMEM((16, 128), f32),
            pltpu.VMEM((n_rep - 1, 16, 128), f32),
            pltpu.VMEM((n_rep, 16, 128), f32),
            pltpu.VMEM((8, 128), f32),
            pltpu.VMEM((n_fsdp - 1, 8, 128), f32),
            dma((8,)),
            dma((14,)),
            dma((14,)),
            dma((8,)),
            dma((8,)),
            dma((8,)),
            dma((8,)),
            dma((5,)),
            dma((5,)),
            pltpu.SemaphoreType.REGULAR,
        ],
        compiler_params=pltpu.CompilerParams(collective_id=0, has_side_effects=True, vmem_limit_bytes=40 * 1024 * 1024),
        name="step",
    )(
        *(
            pltpu.with_memory_space_constraint(a, pltpu.HBM)
            for a in (
                tokens[0],
                norm_gain.reshape(64, 128),
                weights[0],
                first_moment[0],
                second_moment[0],
                upstream[0],
                global_params,
                outer_momentum,
            )
        ),
        fragment,
    )
    out = pl.pallas_call(
        hand_over,
        out_shape=tuple(pltpu.HBM(o.shape, o.dtype) for o in out),
        in_specs=[vm] * 4,
        out_specs=(anywhere,) * 4,
        scratch_shapes=[dma((4,))],
        name="hand_over",
    )(*(pltpu.with_memory_space_constraint(o, pltpu.VMEM) for o in out))
    return (out[0][None], out[1][None], out[2], out[3])


def solution(mesh):
    placed = (
        P("rep", "fsdp", None),
        P(),
        P("rep", "fsdp", None),
        P("rep", "fsdp", None),
        P("rep", "fsdp", None),
        P("rep", "fsdp", None),
        P(None, "fsdp", "rep", None),
        P(None, "fsdp", "rep", None),
        P(),
    )
    return jax.shard_map(
        functools.partial(per_device, mesh.shape["rep"], mesh.shape["fsdp"]),
        mesh=mesh,
        in_specs=placed,
        out_specs=(
            P("rep", "fsdp", None),
            P("rep", "fsdp", None),
            P(None, "fsdp", "rep", None),
            P(None, "fsdp", "rep", None),
        ),
        check_vma=False,
    )
```

```python
import functools

import jax
import jax.numpy as jnp
from jax import lax
from jax.experimental import pallas as pl
from jax.experimental.pallas import tpu as pltpu
from jax.sharding import PartitionSpec as P

MESH = pl.DeviceIdType.MESH

clip_bound = 1.0
inner_rate = 0.02
decay_rate = 0.1
outer_rate = 0.7
outer_mom = 0.9
blend = 0.5

ORDER = (1, 7, 2, 6, 3, 5, 4)
AHEAD, BACK = (0, 1, 3, 5, 7), (0, 2, 4, 6, 7)


def kernel(
    n_rep,
    nz,
    tok_hbm,
    gain_hbm,
    w_hbm,
    fm_hbm,
    sm_hbm,
    u_hbm,
    gp_hbm,
    mom_hbm,
    frag_ref,
    nw,
    val,
    ng_ref,
    nm_ref,
    x,
    xn,
    tp,
    to,
    w,
    wp,
    u,
    fm,
    sm,
    gain_ref,
    gp_ref,
    mom_ref,
    gown,
    gsend,
    grecv,
    vsend,
    vrecv,
    vown,
    scale_ref,
    wsel,
    wrecv,
    gnew,
    grow,
    gfull,
    nsend,
    nrecv,
    loc,
    t_s,
    t_r,
    u_s,
    u_r,
    v_s,
    v_r,
    one_s,
    one_r,
    hello,
):
    r = lax.axis_index("rep")
    f = lax.axis_index("fsdp")
    y, z = f // nz, f % nz
    n_f = 2 * nz
    rows, feats = 128, 512
    f32, bf16 = jnp.float32, jnp.bfloat16

    def zdev(k):
        return {"rep": r, "fsdp": y * nz + (z + k) % nz}

    partner = {"rep": r, "fsdp": (1 - y) * nz + z}

    def remote(src, dst, send_sem, recv_sem, device):
        return pltpu.make_async_remote_copy(
            src_ref=src, dst_ref=dst, send_sem=send_sem, recv_sem=recv_sem, device_id=device, device_id_type=MESH
        )

    barrier = pltpu.get_barrier_semaphore()

    def greet_f(k, c):
        pl.semaphore_signal(barrier, inc=1, device_id={"rep": r, "fsdp": (f + k) % n_f}, device_id_type=MESH)
        return c

    half, quad = n_rep // 2, n_rep // 8
    rank = (r % 2) * half + (r // 2 % 4) * quad + r // 8

    def at_rank(q):
        return {"rep": (q % quad) * 8 + (q % half) // quad * 2 + q // half, "fsdp": f}

    def greet_r(q, c):
        pl.semaphore_signal(barrier, inc=1, device_id=at_rank(q), device_id_type=MESH)
        return c

    def say_hello(q, c):
        pl.semaphore_signal(hello, inc=1, device_id=at_rank(q), device_id_type=MESH)
        return c

    local = [
        pltpu.make_async_copy(src, dst, loc.at[n])
        for n, (src, dst) in enumerate(
            (
                (u_hbm, u.at[0]),
                (w_hbm, w),
                (tok_hbm, x),
                (gain_hbm, gain_ref),
                (gp_hbm, gp_ref),
                (mom_hbm, mom_ref),
                (fm_hbm, fm),
                (sm_hbm, sm),
            )
        )
    ]
    lax.fori_loop(1, n_f, greet_f, 0)
    for c in local[:3]:
        c.start()
    lax.fori_loop(rank + 1, n_rep, greet_r, 0)
    for c in local[3:]:
        c.start()

    copies = []

    def keep(c):
        c.start()
        copies.append(c)
        return c

    def hop(h):
        part = [slice(0, rows), slice(0, rows)] if h < 4 else [slice(0, rows // 2), slice(rows // 2, rows)]
        return [
            keep(remote(u.at[s[h - 1], p], u.at[s[h], p], u_s.at[2 * h - 2 + n], u_r.at[2 * h - 2 + n], zdev((1, nz - 1)[n])))
            for n, (s, p) in enumerate(zip((AHEAD, BACK), part))
        ]

    local[0].wait()
    pl.semaphore_wait(barrier, n_f - 1 + rank)
    u_in = hop(1)
    local[1].wait()
    w_copy = keep(remote(w, wp, one_s.at[0], one_r.at[0], partner))
    local[2].wait()

    def squares(i, acc):
        for j in range(4):
            v = x[:, pl.ds(pl.multiple_of(i * 512 + j * 128, 128), 128)].astype(f32)
            acc = acc + v * v
        return acc

    acc = lax.fori_loop(0, 2 * nz, squares, jnp.zeros((rows, 128), f32))
    mean = jnp.sum(acc, axis=1, keepdims=True) / (2 * nz * feats)
    scale_ref[...] = jnp.broadcast_to(lax.rsqrt(mean + 1e-05), (rows, 128))

    def normed(block, dst):
        for j in range(4):
            g = gain_ref[pl.ds(block * 4 + j, 1), :]
            v = x[:, pl.ds(pl.multiple_of(block * feats + j * 128, 128), 128)].astype(f32)
            dst[:, j * 128 : (j + 1) * 128] = (v * scale_ref[...] * g).astype(bf16)

    t_in = {}

    def prepare(kind, i):
        block = (1 - y if kind == 0 else y) * nz + (z + ORDER[i - 1]) % nz
        normed(block, xn.at[kind * 7 + i - 1])

    def send_tokens(kind, i):
        n = kind * 7 + i - 1
        t_in[kind, i] = keep(remote(xn.at[n], (to if kind else tp).at[i], t_s.at[n], t_r.at[n], zdev(ORDER[i - 1])))

    def send_rows(k, c):
        dst = (r + k) % n_rep
        remote(wsel.at[dst], wrecv.at[k - 1], one_s.at[1], one_r.at[1], {"rep": dst, "fsdp": f}).start()
        return c

    def wait_all(cs):
        for c in cs:
            c.wait_recv()

    def grad(t, first, count, cols):
        k = count * rows
        return lax.dot_general(
            t[first : first + count, :, cols].reshape(k, -1),
            u[first : first + count].reshape(k, feats),
            (((0,), (0,)), ((), ())),
            preferred_element_type=f32,
        )

    def partial(i):
        return jnp.dot(tp[i], wp[...], preferred_element_type=f32) + jnp.dot(to[i], w[...], preferred_element_type=f32)

    def wait_tokens(*slots):
        for i in slots:
            t_in[0, i].wait_recv()
            t_in[1, i].wait_recv()

    halves = (slice(0, 256), slice(256, 512))
    first_half, last_half = slice(0, rows // 2), slice(rows // 2, rows)

    def ring(at, ahead, back):
        out = []
        for n, part in enumerate((ahead, back)):
            v_in[n].wait_recv()
            if at == 2:
                mine, other = (first_half, last_half)[n], (last_half, first_half)[n]
                vsend[at + n, mine] = (part[mine] + vrecv[0, mine].astype(f32)).astype(bf16)
                vsend[at + n, other] = part[other].astype(bf16)
            else:
                vsend[at + n] = (part + vrecv[at - 2 + n].astype(f32)).astype(bf16)
            out.append(
                keep(remote(vsend.at[at + n], vrecv.at[at + n], v_s.at[at + n], v_r.at[at + n], zdev((1, nz - 1)[n])))
            )
        return out

    local[3].wait()
    for i in (7, 5, 6):
        prepare(0, i)
        send_tokens(0, i)
    frag = frag_ref[0]
    sel = w[:, 0:128]
    for j in range(1, 4):
        sel = jnp.where(frag == j, w[:, j * 128 : (j + 1) * 128], sel)
    wsel[...] = sel.reshape(wsel.shape)
    lax.fori_loop(0, rank, say_hello, 0)
    for i in (3, 4, 1, 2):
        prepare(0, i)

    wait_all(u_in)
    u_in = hop(2)
    send_tokens(0, 3)
    send_tokens(0, 4)
    normed((1 - y) * nz + z, tp.at[0])
    normed(y * nz + z, to.at[0])
    for i in (7, 5, 6):
        prepare(1, i)
    wait_all(u_in)
    u_in = hop(3)
    send_tokens(0, 1)
    send_tokens(0, 2)

    @pl.when(rank < n_rep - 1)
    def _():
        pl.semaphore_wait(hello, n_rep - 1 - rank)

    lax.fori_loop(1, n_rep, send_rows, 0)
    for i in (3, 4, 1, 2):
        prepare(1, i)
    w_copy.wait_recv()
    vown[...] = partial(0)
    wait_all(u_in)
    u_in = hop(4)
    send_tokens(1, 7)
    for i in (7, 5, 6):
        t_in[0, i].wait_recv()
    send_tokens(1, 5)
    send_tokens(1, 6)
    for i in (3, 4, 1, 2):
        t_in[0, i].wait_recv()
    wait_all(u_in)
    for m in halves:
        gsend[m, :] = grad(tp, 0, nz, m).astype(bf16)
    g_copy = keep(remote(gsend, grecv, one_s.at[3], one_r.at[3], partner))
    t_in[1, 7].wait_recv()
    vsend[0] = partial(7).astype(bf16)
    v_in = [
        keep(remote(vsend.at[0, p], vrecv.at[0, p], v_s.at[n], v_r.at[n], zdev((1, nz - 1)[n])))
        for n, p in enumerate((first_half, last_half))
    ]
    for m in halves:
        gown[m, :] = grad(to, 0, 1, m) + grad(to, 7, 1, m)
    send_tokens(1, 3)
    send_tokens(1, 4)
    t_in[1, 6].wait_recv()
    t_in[1, 5].wait_recv()
    v_in = ring(2, partial(6), partial(5))
    pltpu.make_async_copy(wrecv, wrecv, one_r.at[1]).wait()

    def add_rows(k, acc):
        return acc + wrecv[k].astype(f32)

    total_rows = lax.fori_loop(0, n_rep - 1, add_rows, wsel[r].astype(f32))
    local[4].wait()
    local[5].wait()
    share_g, share_u = gp_ref[0, 0], mom_ref[0, 0]
    for j in range(1, 4):
        share_g = jnp.where(frag == j, gp_ref[j, 0], share_g)
        share_u = jnp.where(frag == j, mom_ref[j, 0], share_u)
    delta = share_g - total_rows / n_rep
    u_new = outer_mom * share_u + delta
    g_new = share_g - outer_rate * (outer_mom * u_new + delta)
    gnew[...] = g_new

    def send_new(k, c):
        remote(gnew, grow.at[k - 1], one_s.at[2], one_r.at[2], {"rep": (r + k) % n_rep, "fsdp": f}).start()
        return c

    lax.fori_loop(1, n_rep, send_new, 0)
    for j in range(4):
        ng_ref[j, 0] = jnp.where(frag == j, g_new, gp_ref[j, 0])
        nm_ref[j, 0] = jnp.where(frag == j, u_new, mom_ref[j, 0])

    for m in halves:
        gown[m, :] += grad(to, 5, 2, m)
    t_in[1, 4].wait_recv()
    t_in[1, 3].wait_recv()
    send_tokens(1, 1)
    send_tokens(1, 2)
    v_in = ring(4, partial(4), partial(3))
    for m in halves:
        gown[m, :] += grad(to, 3, 2, m)
    t_in[1, 1].wait_recv()
    t_in[1, 2].wait_recv()
    g_copy.wait_recv()
    acc = jnp.zeros((8, feats), f32)
    for m in halves:
        g = gown[m, :] + grecv[m, :].astype(f32) + grad(to, 1, 2, m)
        gown[m, :] = g
        acc = acc + jnp.sum((g * g).reshape(32, 8, feats), axis=0)
    nsend[...] = acc[:, 0:128] + acc[:, 128:256] + acc[:, 256:384] + acc[:, 384:512]

    def send_norm(k, c):
        remote(nsend, nrecv.at[k - 1], one_s.at[4], one_r.at[4], {"rep": r, "fsdp": (f + k) % n_f}).start()
        return c

    lax.fori_loop(1, n_f, send_norm, 0)

    v_in = ring(6, partial(2), partial(1))
    pltpu.make_async_copy(grow, grow, one_r.at[2]).wait()
    gfull[r] = gnew[...]

    def place(k, c):
        gfull[(r + n_rep - k) % n_rep] = grow[k - 1]
        return c

    lax.fori_loop(1, n_rep, place, 0)

    local[6].wait()
    local[7].wait()
    pltpu.make_async_copy(nrecv, nrecv, one_r.at[4]).wait()
    tile = nsend[...] + jnp.sum(nrecv[...], axis=0)
    total = jnp.sum(jnp.sum(tile, axis=1, keepdims=True), axis=0, keepdims=True)
    factor = jnp.minimum(1.0, clip_bound / (jnp.sqrt(total) + 1e-06))

    def update(i, c):
        at = pl.ds(pl.multiple_of(i * 64, 64), 64)
        rows_new = gfull[pl.ds(i * 4, 4)].reshape(64, 128)
        for j in range(4):
            cols = slice(j * 128, (j + 1) * 128)
            clipped = gown[at, cols] * factor
            moment = 0.9 * fm[at, cols].astype(f32) + 0.1 * clipped
            square = 0.95 * sm[at, cols].astype(f32) + 0.05 * clipped * clipped
            wf = w[at, cols].astype(f32)
            inner = wf - inner_rate * (moment / (jnp.sqrt(square) + 1e-08) + decay_rate * wf)
            merged = blend * inner + (1.0 - blend) * rows_new
            nw[at, cols] = jnp.where(frag == j, merged, inner).astype(bf16)
        return c

    lax.fori_loop(0, 8, update, 0)

    wait_all(v_in)
    val[...] = (vown[...] + vrecv[6].astype(f32) + vrecv[7].astype(f32)).astype(bf16)

    for c in copies:
        c.wait_send()
    pltpu.make_async_copy(wrecv, wrecv, one_s.at[1]).wait()
    pltpu.make_async_copy(grow, grow, one_s.at[2]).wait()
    pltpu.make_async_copy(nrecv, nrecv, one_s.at[4]).wait()


def hand_over(*refs):
    n = len(refs) // 2
    sems = refs[-1]
    copies = [pltpu.make_async_copy(refs[i], refs[n + i], sems.at[i]) for i in range(n)]
    for c in copies:
        c.start()
    for c in copies:
        c.wait()


def per_device(n_rep, n_fsdp, tokens, norm_gain, weights, first_moment, second_moment, upstream, global_params, outer_momentum, fragment):
    nz = n_fsdp // 2
    bf, f32 = jnp.bfloat16, jnp.float32
    vm, anywhere = pl.BlockSpec(memory_space=pltpu.VMEM), pl.BlockSpec(memory_space=pl.ANY)
    dma = pltpu.SemaphoreType.DMA
    out = pl.pallas_call(
        functools.partial(kernel, n_rep, nz),
        out_shape=(
            pltpu.VMEM((512, 512), bf),
            pltpu.VMEM((128, 512), bf),
            pltpu.VMEM(global_params.shape, f32),
            pltpu.VMEM(outer_momentum.shape, f32),
        ),
        in_specs=[anywhere] * 8 + [pl.BlockSpec(memory_space=pltpu.SMEM)],
        out_specs=(vm,) * 4,
        scratch_shapes=[
            pltpu.VMEM((128, 8192), bf),
            pltpu.VMEM((14, 128, 512), bf),
            pltpu.VMEM((8, 128, 512), bf),
            pltpu.VMEM((8, 128, 512), bf),
            pltpu.VMEM((512, 512), bf),
            pltpu.VMEM((512, 512), bf),
            pltpu.VMEM((8, 128, 512), bf),
            pltpu.VMEM((512, 512), bf),
            pltpu.VMEM((512, 512), bf),
            pltpu.VMEM((64, 128), f32),
            pltpu.VMEM(global_params.shape, f32),
            pltpu.VMEM(outer_momentum.shape, f32),
            pltpu.VMEM((512, 512), f32),
            pltpu.VMEM((512, 512), bf),
            pltpu.VMEM((512, 512), bf),
            pltpu.VMEM((8, 128, 512), bf),
            pltpu.VMEM((8, 128, 512), bf),
            pltpu.VMEM((128, 512), f32),
            pltpu.VMEM((128, 128), f32),
            pltpu.VMEM((n_rep, 16, 128), bf),
            pltpu.VMEM((n_rep - 1, 16, 128), bf),
            pltpu.VMEM((16, 128), f32),
            pltpu.VMEM((n_rep - 1, 16, 128), f32),
            pltpu.VMEM((n_rep, 16, 128), f32),
            pltpu.VMEM((8, 128), f32),
            pltpu.VMEM((n_fsdp - 1, 8, 128), f32),
            dma((8,)),
            dma((14,)),
            dma((14,)),
            dma((8,)),
            dma((8,)),
            dma((8,)),
            dma((8,)),
            dma((5,)),
            dma((5,)),
            pltpu.SemaphoreType.REGULAR,
        ],
        compiler_params=pltpu.CompilerParams(collective_id=0, has_side_effects=True, vmem_limit_bytes=40 * 1024 * 1024),
        name="step",
    )(
        *(
            pltpu.with_memory_space_constraint(a, pltpu.HBM)
            for a in (
                tokens[0],
                norm_gain.reshape(64, 128),
                weights[0],
                first_moment[0],
                second_moment[0],
                upstream[0],
                global_params,
                outer_momentum,
            )
        ),
        fragment,
    )
    out = pl.pallas_call(
        hand_over,
        out_shape=tuple(pltpu.HBM(o.shape, o.dtype) for o in out),
        in_specs=[vm] * 4,
        out_specs=(anywhere,) * 4,
        scratch_shapes=[dma((4,))],
        name="hand_over",
    )(*(pltpu.with_memory_space_constraint(o, pltpu.VMEM) for o in out))
    return (out[0][None], out[1][None], out[2], out[3])


def solution(mesh):
    placed = (
        P("rep", "fsdp", None),
        P(),
        P("rep", "fsdp", None),
        P("rep", "fsdp", None),
        P("rep", "fsdp", None),
        P("rep", "fsdp", None),
        P(None, "fsdp", "rep", None),
        P(None, "fsdp", "rep", None),
        P(),
    )
    return jax.shard_map(
        functools.partial(per_device, mesh.shape["rep"], mesh.shape["fsdp"]),
        mesh=mesh,
        in_specs=placed,
        out_specs=(
            P("rep", "fsdp", None),
            P("rep", "fsdp", None),
            P(None, "fsdp", "rep", None),
            P(None, "fsdp", "rep", None),
        ),
        check_vma=False,
    )
```
